512 devices in a mesh: seq: 64 (over y_hi, z, core), head: 8 (over y_lo, x).
Axes of the slice: x: 4, y: 4 (y_hi: 2, y_lo: 2; y = y_hi * 2 + y_lo), z: 16, core: 2. Of those that a mesh axis runs over, the one named last changes fastest.
Arguments:
- queries: bfloat16 [8192, 8192], P('seq', 'head'), may hold values from -6 to 6
- keys: bfloat16 [8192, 1024], P('seq', 'head'), may hold values from -6 to 6
- values: bfloat16 [8192, 1024], P('seq', 'head'), may hold values from -6 to 6
- layout: int32 [64], replicated, may hold values from 0 to 63, as said below
Outputs:
- attended: bfloat16 [8192, 8192], P(('seq', 'head'))
The draws below stay inside these ranges and needn't reach their ends.
Inputs may be any that keep to these rules, and one draw needn't show every extreme that they name: `layout`: the first 32 entries hold each block below 32 once; entry 32 + i equals 63 - entry i.
All inputs are finite; a program needn't handle non-finite values.
Results may differ from the reference program's by a relative error of at most 0.007.
Values may be sent and summed in bfloat16 or wider, within the bound.
A program may use at most 128 MiB of HBM per device.

```python
import jax
import jax.numpy as jnp
from jax import lax

QUERY_HEADS = 64
KEY_VALUE_HEADS = 8
HEAD_SIZE = 128
TOK_DEV = 128
NBLK = 64
SEQUENCE_TOKENS = 8192


def draw_queries(key, part):
    key = jax.random.fold_in(key, 11)
    return jnp.clip(jax.random.normal(key, (SEQUENCE_TOKENS, QUERY_HEADS * HEAD_SIZE), jnp.float32), -5.5, 5.5).astype(jnp.bfloat16)


def draw_keys(key, part):
    key = jax.random.fold_in(key, 23)
    return jnp.clip(jax.random.normal(key, (SEQUENCE_TOKENS, KEY_VALUE_HEADS * HEAD_SIZE), jnp.float32), -5.5, 5.5).astype(jnp.bfloat16)


def draw_layout(key, part):
    key = jax.random.fold_in(key, 37)
    early = jax.random.permutation(key, NBLK // 2).astype(jnp.int32)
    return jnp.concatenate([early, NBLK - 1 - early]).astype(jnp.int32)


def levels(rng, dims, shards, low, high):
    gain, own = 1.0, jax.random.fold_in(rng, 6)
    for dim, blocks in shards:
        draws = jnp.exp(jax.random.uniform(jax.random.fold_in(own, dim), (blocks,), jnp.float32, low / len(shards), high / len(shards)))
        gain = gain * jnp.repeat(draws, dims[dim] // blocks).reshape([-1 if axis == dim else 1 for axis in range(len(dims))])
    return gain


def gaussian(own_key, shape, scale, limit, shards=(), held_as=jnp.bfloat16):
    entries = scale * jax.random.normal(own_key, shape, jnp.float32)
    if shards:
        entries = entries * levels(own_key, shape, shards, -0.22, 0.18)
    return jnp.clip(entries, -limit, limit).astype(held_as)


def setup_inputs(seed: int = 0) -> dict:
    key_of = jax.random.split(jax.random.key(seed), 5)
    return {
        "queries": draw_queries(jax.random.fold_in(key_of[4], 71), 0),
        "keys": draw_keys(jax.random.fold_in(key_of[4], 71), 0),
        "values": gaussian(key_of[2], (SEQUENCE_TOKENS, KEY_VALUE_HEADS * HEAD_SIZE), 1.0, 6.0, ((0, 64), (1, 8))),
        "layout": draw_layout(jax.random.fold_in(key_of[4], 71), 0),
    }


def reference(queries, keys, values, layout):
    rows = jnp.arange(SEQUENCE_TOKENS, dtype=jnp.int32)
    position = (layout[rows // TOK_DEV] * TOK_DEV + rows % TOK_DEV).astype(jnp.int32)
    query_group = QUERY_HEADS // KEY_VALUE_HEADS
    q_heads = queries.reshape(SEQUENCE_TOKENS, QUERY_HEADS, HEAD_SIZE).transpose(1, 0, 2).reshape(QUERY_HEADS, SEQUENCE_TOKENS // TOK_DEV, TOK_DEV, HEAD_SIZE)
    key_head_rows = keys.reshape(SEQUENCE_TOKENS, KEY_VALUE_HEADS, HEAD_SIZE).transpose(1, 0, 2)
    value_head_rows = values.reshape(SEQUENCE_TOKENS, KEY_VALUE_HEADS, HEAD_SIZE).transpose(1, 0, 2)
    q_pos = position.reshape(SEQUENCE_TOKENS // TOK_DEV, TOK_DEV)

    def per_head(item):
        q_head, kv_index = item
        k_head = lax.dynamic_index_in_dim(key_head_rows, kv_index, 0, keepdims=False)
        v_head = lax.dynamic_index_in_dim(value_head_rows, kv_index, 0, keepdims=False)

        def per_block(block):
            q_block, pos_block = block
            score = jnp.dot(q_block, k_head.T, preferred_element_type=jnp.float32) * (HEAD_SIZE ** -0.5)
            allowed = position[None, :] <= pos_block[:, None]
            score = jnp.where(allowed, score, jnp.float32(-1e30))
            top = jnp.max(score, axis=1, keepdims=True)
            weight = jnp.where(allowed, jnp.exp(score - top), jnp.float32(0.0))
            total = jnp.sum(weight, axis=1, keepdims=True)
            mixed = jnp.dot(weight.astype(jnp.bfloat16), v_head, preferred_element_type=jnp.float32)
            return (mixed / total).astype(jnp.bfloat16)

        return lax.map(per_block, (q_head, q_pos))

    heads_index = (jnp.arange(QUERY_HEADS, dtype=jnp.int32) // query_group).astype(jnp.int32)
    result = lax.map(per_head, (q_heads, heads_index))
    return result.reshape(QUERY_HEADS, SEQUENCE_TOKENS, HEAD_SIZE).transpose(1, 0, 2).reshape(SEQUENCE_TOKENS, QUERY_HEADS * HEAD_SIZE)
```

```python
import math

import jax
import jax.numpy as jnp
from jax import lax
from jax.experimental import pallas as pl
from jax.experimental.pallas import tpu as pltpu
from jax.sharding import PartitionSpec as P


HEAD_SIZE = 128
MESH = pl.DeviceIdType.MESH
EMPTY = -1e30
SCALE = math.log2(math.e) / math.sqrt(HEAD_SIZE)
TILE = 4
CHUNKS = 2


def kernel(
    nz, heads, layout_ref, q_ref, k_ref, v_ref, out_ref,
    kv, qx, relay, qs, m_s, al_s, out_send, out_recv, stat_send, stat_recv, lse, pick, limit, place,
    ring_send, ring_recv, share_send, share_recv, cross_send, cross_recv,
    first_send, first_recv, second_send, second_recv, o_send, o_recv,
):
    tok, width = q_ref.shape
    group = width // HEAD_SIZE
    per_chunk = group // CHUNKS
    rows = per_chunk * tok
    seq, h = lax.axis_index("seq"), lax.axis_index("head")
    plane, z, core = seq // (2 * nz), (seq // 2) % nz, seq % 2
    nx = heads // 2
    y_lo, x = h // nx, h % nx

    def at(p, zz, cc):
        return (p * nz + zz) * 2 + cc

    right, left = (at(plane, (z + 1) % nz, core), h), (at(plane, (z + nz - 1) % nz, core), h)
    sibling, cross = (at(plane, z, 1 - core), h), (at(1 - plane, z, 1 - core), h)
    above = (at((plane + y_lo) % 2, z, core), (1 - y_lo) * nx + x)
    below = (at((plane + 1 - y_lo) % 2, z, core), (1 - y_lo) * nx + x)

    def outward(e):
        return (plane + e // heads) % 2, (h + e % heads) % heads

    def send(src, dst, send_sem, recv_sem, device):
        return pltpu.make_async_remote_copy(
            src_ref=src, dst_ref=dst, send_sem=send_sem, recv_sem=recv_sem, device_id=device, device_id_type=MESH
        )

    barrier = pltpu.get_barrier_semaphore()
    for device in (right, left, sibling, cross):
        pl.semaphore_signal(barrier, inc=1, device_id=device, device_id_type=MESH)
    for e in range(1, 2 * heads):
        p, j = outward(e)
        pl.semaphore_signal(barrier, inc=1, device_id=(at(p, z, core), j), device_id_type=MESH)
    pl.semaphore_wait(barrier, 4 + 2 * heads - 1)

    def ring(way, d, g):
        src, dst, device = (d - 1, d, right) if way == 0 else ((nz - d + 1) % nz, nz - d, left)
        return send(kv.at[src, core, g], kv.at[dst, core, g], ring_send.at[dst, g], ring_recv.at[dst, g], device)

    def share(slot, g):
        return send(kv.at[slot, core, g], kv.at[slot, core, g], share_send.at[slot, g], share_recv.at[slot, g], sibling)

    def shared(slot, g):
        ref = kv.at[slot, 1 - core, g]
        return send(ref, ref, share_send.at[slot, g], share_recv.at[slot, g], sibling)

    def exchange(g):
        return send((k_ref, v_ref)[g], kv.at[0, 1 - core, g], cross_send.at[g], cross_recv.at[g], cross)

    def exchanged(g):
        return send((k_ref, v_ref)[g], kv.at[0, core, g], cross_send.at[g], cross_recv.at[g], cross)

    half, strip = width // 2, tok // 2

    def first(way, r):
        src = q_ref.at[pl.ds(r * strip, strip), pl.ds(way * half, half)]
        return send(src, relay.at[way, r], first_send.at[way, r], first_recv.at[way, r], (above, below)[way])

    def second(way, r):
        dst = qx.at[pl.ds(r * strip, strip), pl.ds(way * half, half)]
        return send(relay.at[way, r], dst, second_send.at[way, r], second_recv.at[way, r], (above, below)[way])

    @pl.when(core != plane)
    def _():
        for g in range(2):
            exchange(g).start()

    @pl.when(core == plane)
    def _():
        kv[0, core, 0] = k_ref[...]
        kv[0, core, 1] = v_ref[...]

    for r in range(2):
        for way in range(2):
            first(way, r).start()

    for g in range(2):

        @pl.when(core != plane)
        def _():
            exchanged(g).wait_recv()

        for way in range(2):
            ring(way, 1, g).start()
        share(0, g).start()

    tiles = nz // TILE + 1
    own = layout_ref[2 * z + core]
    below_count = jnp.int32(0)
    for i in range(nz):
        below_count += (layout_ref[2 * ((z + nz - i) % nz) + plane] <= own).astype(jnp.int32)
    low_tiles = (below_count + TILE - 1) // TILE
    low_next, high_next = jnp.int32(0), low_tiles * TILE
    for i in range(nz):
        position = layout_ref[2 * ((z + nz - i) % nz) + plane]
        is_low, is_high = position <= own, position >= own
        place[0, i] = jnp.where(is_low, low_next, -1)
        place[1, i] = jnp.where(is_high, high_next, -1)
        place[2, i] = jnp.where(position == own, 0, tok)
        low_next += is_low.astype(jnp.int32)
        high_next += is_high.astype(jnp.int32)

    def order(t, _):
        slot, bound = jnp.int32(0), jnp.int32(-tok)
        for i in range(nz):
            here = (place[0, i] == t) | (place[1, i] == t)
            slot = jnp.where(here, i, slot)
            bound = jnp.where(here, place[2, i], bound)
        pick[t] = slot
        limit[t] = bound
        return 0

    lax.fori_loop(0, tiles * TILE, order, 0)

    def scaled(target, ref):
        for head in range(group):
            block = ref[:, head * HEAD_SIZE:(head + 1) * HEAD_SIZE].astype(jnp.float32) * SCALE
            chunk, start = head // per_chunk, (head % per_chunk) * tok
            qs[target, chunk, start:start + tok, :] = block.astype(jnp.bfloat16)

    scaled(plane, q_ref)

    ones = jnp.ones((TILE * tok, HEAD_SIZE), jnp.bfloat16)

    def update(q, keys, values, m, al, bounds):
        score = lax.dot_general(q, keys, (((1,), (1,)), ((), ())), preferred_element_type=jnp.float32)
        if bounds is not None:
            ahead = lax.broadcasted_iota(jnp.int32, (rows, tok), 1) - lax.rem(
                lax.broadcasted_iota(jnp.int32, (rows, tok), 0), tok
            )
            score = jnp.concatenate(
                [
                    jnp.where(ahead <= bounds[j], score[:, j * tok:(j + 1) * tok], EMPTY)
                    for j in range(TILE)
                ],
                axis=1,
            )
        m_next = jnp.maximum(m, jnp.max(score, axis=1, keepdims=True))
        weight = jnp.exp2(score - jnp.concatenate([m_next] * TILE, axis=1)).astype(jnp.bfloat16)
        mixed = jnp.dot(weight, jnp.concatenate([values, ones], axis=1), preferred_element_type=jnp.float32)
        factor = jnp.exp2(m - m_next)
        return m_next, al * jnp.concatenate([factor, factor], axis=1) + mixed

    def first_part(slots, fresh):
        keys = jnp.concatenate([kv[i, 0, 0] for i in slots], axis=0)
        values = jnp.concatenate([kv[i, 0, 1] for i in slots], axis=0)

        def chunk_step(chunk, _):
            if fresh:
                m = jnp.full((rows, HEAD_SIZE), EMPTY, jnp.float32)
                al = jnp.zeros((rows, 2 * HEAD_SIZE), jnp.float32)
                m_s[0, chunk] = m
                al_s[0, chunk] = al
            else:
                m, al = m_s[1, chunk], al_s[1, chunk]
            m, al = update(qs[1, chunk], keys, values, m, al, None)
            m_s[1, chunk] = m
            al_s[1, chunk] = al
            return 0

        lax.fori_loop(0, CHUNKS, chunk_step, 0)

    arrival = [0] + [i for d in range(1, nz // 2) for i in (d, nz - d)] + [nz // 2]
    parts = [arrival[i:i + TILE] for i in range(0, nz, TILE)]
    last = nz // 2

    def run_part(index):
        for slot in parts[index]:
            for g in range(2):
                shared(slot, g).wait_recv()
        first_part(parts[index], index == 0)

    start_at = last - len(parts) + 1
    for d in range(1, last + 1):
        for g in range(2):
            if d < last:
                for way in range(2):
                    ring(way, d, g).wait_recv()
                    if d + 1 < last:
                        ring(way, d + 1, g).start()
                    else:

                        @pl.when(core == way)
                        def _():
                            ring(way, d + 1, g).start()

                    share(d if way == 0 else nz - d, g).start()
            else:
                ring(0, d, g).wait_recv()
                share(d, g).start()
        if d <= 2:
            for way in range(2):
                first(way, d - 1).wait_recv()
                second(way, d - 1).start()
        if d == start_at - 1:
            for r in range(2):
                for way in range(2):
                    second(way, r).wait_recv()
            scaled(1 - plane, qx)
        if d >= start_at:
            run_part(d - start_at)

    lane = lax.broadcasted_iota(jnp.int32, (tok, HEAD_SIZE), 1)
    piece = tok // heads

    def spread(buffer, landing, index):
        for e in range(1, 2 * heads):
            p, j = outward(e)
            send(
                buffer.at[p * heads + j], landing.at[plane * heads + h], o_send.at[index], o_recv.at[index],
                (at(p, z, core), j),
            ).start()
        mine = plane * heads + h
        pltpu.make_async_copy(buffer.at[mine], landing.at[mine], o_recv.at[index]).start()

    def chunk_step(chunk, _):
        for t in range(tiles):
            is_low = t < low_tiles
            side = jnp.where(is_low, 0, 1)
            before = jnp.where(t == low_tiles, 1, 0 if t == 0 else t + 1)
            slots = [pick[t * TILE + j] for j in range(TILE)]
            bounds = [limit[t * TILE + j] for j in range(TILE)]
            keys = jnp.concatenate([kv[i, side, 0] for i in slots], axis=0)
            values = jnp.concatenate([kv[i, side, 1] for i in slots], axis=0)
            m, al = update(qs[side, chunk], keys, values, m_s[before, chunk], al_s[before, chunk], bounds)
            m_s[2 + t, chunk] = m
            al_s[2 + t, chunk] = al
        for side in range(2):
            end = jnp.where(low_tiles == 0, 0, low_tiles + 1) if side == 0 else tiles + 1
            m, al = m_s[end, chunk], al_s[end, chunk]
            total = al[:, HEAD_SIZE:]
            some = total > 0.0
            safe = jnp.where(some, total, 1.0)
            mixed = (al[:, :HEAD_SIZE] / safe).astype(jnp.bfloat16)
            level = jnp.where(some, m + jnp.log2(safe), EMPTY)
            for k in range(per_chunk):
                block = mixed[k * tok:(k + 1) * tok].reshape(heads, piece, HEAD_SIZE)
                out_send[chunk, side * heads:(side + 1) * heads, :, k * HEAD_SIZE:(k + 1) * HEAD_SIZE] = block
                here = lax.rem(lane, group) == chunk * per_chunk + k
                lse[side] = jnp.where(here, level[k * tok:(k + 1) * tok], lse[side])
        spread(out_send.at[chunk], out_recv.at[chunk], chunk)
        return 0

    lse[...] = jnp.zeros_like(lse)
    lax.fori_loop(0, CHUNKS, chunk_step, 0)

    for side in range(2):
        level = lse[side]
        high = level.astype(jnp.bfloat16).astype(jnp.float32)
        middle = (level - high).astype(jnp.bfloat16).astype(jnp.float32)
        low = level - high - middle
        packed = jnp.where(lane < group, high, jnp.where(lane < 2 * group, middle, low)).astype(jnp.bfloat16)
        stat_send[side * heads:(side + 1) * heads] = packed.reshape(heads, piece, HEAD_SIZE)
    spread(stat_send, stat_recv, CHUNKS)

    for g in range(2):

        @pl.when(core != plane)
        def _():
            exchange(g).wait_send()

        for slot in range(nz):
            share(slot, g).wait_send()
        for d in range(1, last):
            for way in range(2):
                ring(way, d, g).wait_send()
        ring(0, last, g).wait_send()
    for r in range(2):
        for way in range(2):
            first(way, r).wait_send()
            second(way, r).wait_send()

    pltpu.make_async_copy(stat_send, stat_recv, o_recv.at[CHUNKS]).wait()
    for chunk in range(CHUNKS):
        pltpu.make_async_copy(out_send.at[chunk], out_recv.at[chunk], o_recv.at[chunk]).wait()

    for source in range(heads):
        levels = []
        for side in range(2):
            packed = stat_recv[side * heads + source].astype(jnp.float32)
            levels.append(
                packed + pltpu.roll(packed, HEAD_SIZE - group, 1) + pltpu.roll(packed, HEAD_SIZE - 2 * group, 1)
            )
        share_0 = 1.0 / (1.0 + jnp.exp2(levels[1] - levels[0]))
        for head in range(group):
            chunk, k = head // per_chunk, head % per_chunk
            columns = slice(k * HEAD_SIZE, (k + 1) * HEAD_SIZE)
            part_0 = out_recv[chunk, source, :, columns].astype(jnp.float32)
            part_1 = out_recv[chunk, heads + source, :, columns].astype(jnp.float32)
            portion = jnp.broadcast_to(share_0[:, head:head + 1], (piece, HEAD_SIZE))
            start = (source * group + head) * HEAD_SIZE
            out_ref[:, start:start + HEAD_SIZE] = (part_1 + portion * (part_0 - part_1)).astype(jnp.bfloat16)

    others = pl.ds(0, 2 * heads - 1)
    pltpu.make_async_copy(stat_send.at[others], stat_recv.at[others], o_send.at[CHUNKS]).wait()
    for chunk in range(CHUNKS):
        pltpu.make_async_copy(out_send.at[chunk, others], out_recv.at[chunk, others], o_send.at[chunk]).wait()


def solution(mesh):
    nz, heads = mesh.shape["seq"] // 4, mesh.shape["head"]

    def per_device(queries, keys, values, layout):
        tok, width = queries.shape
        group = width // HEAD_SIZE
        rows, piece = group // CHUNKS * tok, tok // heads
        tiles = nz // TILE + 1
        bf16, dma = jnp.bfloat16, pltpu.SemaphoreType.DMA
        vmem = pl.BlockSpec(memory_space=pltpu.VMEM)

        def body(*refs):
            kernel(nz, heads, *refs)

        return pl.pallas_call(
            body,
            out_shape=jax.ShapeDtypeStruct((piece, heads * width), bf16),
            in_specs=[pl.BlockSpec(memory_space=pltpu.SMEM), vmem, vmem, vmem],
            out_specs=vmem,
            scratch_shapes=[
                pltpu.VMEM((nz, 2, 2, tok, HEAD_SIZE), bf16),
                pltpu.VMEM((tok, width), bf16),
                pltpu.VMEM((2, 2, tok // 2, width // 2), bf16),
                pltpu.VMEM((2, CHUNKS, rows, HEAD_SIZE), bf16),
                pltpu.VMEM((tiles + 2, CHUNKS, rows, HEAD_SIZE), jnp.float32),
                pltpu.VMEM((tiles + 2, CHUNKS, rows, 2 * HEAD_SIZE), jnp.float32),
                pltpu.VMEM((CHUNKS, 2 * heads, piece, width // CHUNKS), bf16),
                pltpu.VMEM((CHUNKS, 2 * heads, piece, width // CHUNKS), bf16),
                pltpu.VMEM((2 * heads, piece, HEAD_SIZE), bf16),
                pltpu.VMEM((2 * heads, piece, HEAD_SIZE), bf16),
                pltpu.VMEM((2, tok, HEAD_SIZE), jnp.float32),
                pltpu.SMEM((tiles * TILE,), jnp.int32),
                pltpu.SMEM((tiles * TILE,), jnp.int32),
                pltpu.SMEM((3, nz), jnp.int32),
                dma((nz, 2)), dma((nz, 2)), dma((nz, 2)), dma((nz, 2)),
                dma((2,)), dma((2,)),
                dma((2, 2)), dma((2, 2)), dma((2, 2)), dma((2, 2)),
                dma((CHUNKS + 1,)), dma((CHUNKS + 1,)),
            ],
            compiler_params=pltpu.CompilerParams(
                collective_id=0, has_side_effects=True, vmem_limit_bytes=48 * 1024 * 1024
            ),
            cost_estimate=pl.CostEstimate(
                flops=4 * 2 * (nz + 1) * tok * group * tok * HEAD_SIZE,
                bytes_accessed=4 * tok * width,
                transcendentals=2 * (nz + 1) * tok * group * tok,
            ),
        )(layout, queries, keys, values)

    return jax.shard_map(
        per_device,
        mesh=mesh,
        in_specs=(P("seq", "head"), P("seq", "head"), P("seq", "head"), P()),
        out_specs=P(("seq", "head"), None),
        check_vma=False,
    )
```

```python
import math

import jax
import jax.numpy as jnp
from jax import lax
from jax.experimental import pallas as pl
from jax.experimental.pallas import tpu as pltpu
from jax.sharding import PartitionSpec as P


HEAD_SIZE = 128
MESH = pl.DeviceIdType.MESH
EMPTY = -1e30
SCALE = math.log2(math.e) / math.sqrt(HEAD_SIZE)
CHUNKS = 2
TILE = 4


def places(nz, heads):
    seq, h = lax.axis_index("seq"), lax.axis_index("head")
    return seq // (2 * nz), (seq // 2) % nz, seq % 2, h


def send(src, dst, send_sem, recv_sem, device):
    return pltpu.make_async_remote_copy(
        src_ref=src, dst_ref=dst, send_sem=send_sem, recv_sem=recv_sem, device_id=device, device_id_type=MESH
    )


def kernel(
    nz, heads, groups, layout_hbm, q_hbm, k_ref, v_ref, out_ref,
    kv_0, kv_1, kv_2, q_ref, qx, relay, qs, m_s, al_s, out_send, out_recv, stat_send, stat_recv, lse,
    layout_ref, pick, limit, place,
    ring_send, ring_recv, share_send, share_recv, cross_send, cross_recv,
    first_send, first_recv, second_send, second_recv, o_send, o_recv, local,
):
    tok, width = q_ref.shape
    group = width // HEAD_SIZE
    per_chunk = group // CHUNKS
    piece = tok // heads
    plane, z, core, h = places(nz, heads)
    nx = heads // 2
    y_lo, x = h // nx, h % nx
    last = nz // 2

    def at(p, zz, cc):
        return (p * nz + zz) * 2 + cc

    right, left = (at(plane, (z + 1) % nz, core), h), (at(plane, (z + nz - 1) % nz, core), h)
    sibling, cross = (at(plane, z, 1 - core), h), (at(1 - plane, z, 1 - core), h)
    above = (at((plane + y_lo) % 2, z, core), (1 - y_lo) * nx + x)
    below = (at((plane + 1 - y_lo) % 2, z, core), (1 - y_lo) * nx + x)

    def outward(e):
        return (plane + e // heads) % 2, (h + e % heads) % heads

    def device(e):
        p, j = outward(e)
        return at(p, z, core), j

    where = {slot: (buffer, n) for buffer, slots in zip((kv_0, kv_1, kv_2), groups) for n, slot in enumerate(slots)}

    def block(slot, whose, g=None):
        buffer, n = where[slot]
        return buffer.at[n, whose] if g is None else buffer.at[n, whose, g]

    def own(g):
        return pltpu.make_async_copy((k_ref, v_ref)[g], block(0, core, g), local.at[g])

    loads = (
        pltpu.make_async_copy(q_hbm, q_ref, local.at[2]),
        pltpu.make_async_copy(layout_hbm, layout_ref, local.at[3]),
    )

    @pl.when(core == plane)
    def _():
        for g in range(2):
            own(g).start()

    for load in loads:
        load.start()

    barrier = pltpu.get_barrier_semaphore()
    around = [right, left, sibling, cross] + [device(e) for e in range(1, 2 * heads)]
    for to in around:
        pl.semaphore_signal(barrier, inc=1, device_id=to, device_id_type=MESH)
    pl.semaphore_wait(barrier, len(around))

    def ring(way, d, g):
        src, dst, to = (d - 1, d, right) if way == 0 else ((nz - d + 1) % nz, nz - d, left)
        return send(block(src, core, g), block(dst, core, g), ring_send.at[dst, g], ring_recv.at[dst, g], to)

    def share(slot, whose):
        ref = block(slot, whose)
        return send(ref, ref, share_send.at[slot], share_recv.at[slot], sibling)

    def cross_copy(g, whose):
        return send((k_ref, v_ref)[g], block(0, whose, g), cross_send.at[g], cross_recv.at[g], cross)

    half, strip = width // 2, tok // 2

    def first(way, r):
        src = q_hbm.at[pl.ds(r * strip, strip), pl.ds(way * half, half)]
        return send(src, relay.at[way, r], first_send.at[way, r], first_recv.at[way, r], (above, below)[way])

    def second(way, r):
        dst = qx.at[pl.ds(r * strip, strip), pl.ds(way * half, half)]
        return send(relay.at[way, r], dst, second_send.at[way, r], second_recv.at[way, r], (above, below)[way])

    @pl.when(core != plane)
    def _():
        for g in range(2):
            cross_copy(g, 1 - core).start()

    for g in range(2):

        @pl.when(core != plane)
        def _():
            cross_copy(g, core).wait_recv()

        @pl.when(core == plane)
        def _():
            own(g).wait()

        for way in range(2):
            ring(way, 1, g).start()
    share(0, core).start()
    for r in range(2):
        for way in range(2):
            first(way, r).start()
    for load in loads:
        load.wait()

    own_block = layout_ref[2 * z + core]
    low_tiles, starts, tile_counts = [], [], []
    start = 0
    for slots in groups:
        tiles = len(slots) // TILE + 1
        positions = [layout_ref[2 * ((z + nz - slot) % nz) + plane] for slot in slots]
        count = jnp.int32(0)
        for position in positions:
            count += (position <= own_block).astype(jnp.int32)
        low = (count + TILE - 1) // TILE
        low_next, high_next = jnp.int32(0), low * TILE
        for n, position in enumerate(positions):
            is_low, is_high = position <= own_block, position >= own_block
            place[0, n] = jnp.where(is_low, low_next, -1)
            place[1, n] = jnp.where(is_high, high_next, -1)
            place[2, n] = jnp.where(position == own_block, 0, tok)
            low_next += is_low.astype(jnp.int32)
            high_next += is_high.astype(jnp.int32)

        def order(t, _):
            index, bound = jnp.int32(0), jnp.int32(-tok)
            for n in range(len(slots)):
                here = (place[0, n] == t) | (place[1, n] == t)
                index = jnp.where(here, n, index)
                bound = jnp.where(here, place[2, n], bound)
            pick[start + t] = index
            limit[start + t] = bound
            return 0

        lax.fori_loop(0, tiles * TILE, order, 0)
        low_tiles.append(low)
        starts.append(start)
        tile_counts.append(tiles)
        start += tiles * TILE

    def scaled(target, ref):
        for head in range(group):
            part = ref[:, head * HEAD_SIZE:(head + 1) * HEAD_SIZE].astype(jnp.float32) * SCALE
            qs[target, head] = part.astype(jnp.bfloat16)

    scaled(plane, q_ref)
    ones = jnp.ones((TILE * tok, HEAD_SIZE), jnp.bfloat16)

    def tile(side, keys, values, before, after, bounds, offset, count):
        values = jnp.concatenate([values, ones], axis=1)

        def scores(n):
            return lax.dot_general(
                qs[side, offset + n], keys, (((1,), (1,)), ((), ())), preferred_element_type=jnp.float32
            )

        if bounds is not None:
            ahead = lax.broadcasted_iota(jnp.int32, (tok, tok), 1) - lax.broadcasted_iota(jnp.int32, (tok, tok), 0)
        upcoming = scores(0)
        for n in range(count):
            score = upcoming
            if n + 1 < count:
                upcoming = scores(n + 1)
            parts = [score[:, j * tok:(j + 1) * tok] for j in range(TILE)]
            if bounds is not None:
                parts = [jnp.where(ahead <= bounds[j], parts[j], EMPTY) for j in range(TILE)]
            widest = parts[0]
            for part in parts[1:]:
                widest = jnp.maximum(widest, part)
            top = jnp.max(widest, axis=1, keepdims=True)
            if before is None:
                m_next = jnp.broadcast_to(top, (tok, HEAD_SIZE))
            else:
                m = m_s[before, offset + n]
                m_next = jnp.maximum(m, top)
            weight = jnp.concatenate([jnp.exp2(part - m_next).astype(jnp.bfloat16) for part in parts], axis=1)
            mixed = jnp.dot(weight, values, preferred_element_type=jnp.float32)
            if before is not None:
                factor = jnp.exp2(m - m_next)
                mixed += al_s[before, offset + n] * jnp.concatenate([factor, factor], axis=1)
            m_s[after, offset + n] = m_next
            al_s[after, offset + n] = mixed

    m_s[0] = jnp.full(m_s.shape[1:], EMPTY, jnp.float32)
    al_s[0] = jnp.zeros(al_s.shape[1:], jnp.float32)

    def first_part(slots, before, after, offset, count):
        keys = jnp.concatenate([block(slot, 0, 0)[...] for slot in slots], axis=0)
        values = jnp.concatenate([block(slot, 0, 1)[...] for slot in slots], axis=0)
        tile(1, keys, values, before, after, None, offset, count)

    def second_part(index, low_before, high_before, after, offset, count):
        buffer, low, begin = (kv_0, kv_1, kv_2)[index], low_tiles[index], starts[index]

        def step(t, _):
            side = jnp.where(t < low, 0, 1)
            before = jnp.where(t == low, high_before, jnp.where(t == 0, low_before, after + t - 1))
            chosen = [pick[begin + t * TILE + j] for j in range(TILE)]
            bounds = [limit[begin + t * TILE + j] for j in range(TILE)]
            keys = jnp.concatenate([buffer[n, side, 0] for n in chosen], axis=0)
            values = jnp.concatenate([buffer[n, side, 1] for n in chosen], axis=0)
            tile(side, keys, values, before, after + t, bounds, offset, count)
            return 0

        lax.fori_loop(0, tile_counts[index], step, 0)
        return jnp.where(low == 0, low_before, after + low - 1), after + tile_counts[index] - 1

    def arrived(slots):
        for slot in slots:
            share(slot, 1 - core).wait_recv()

    near, middle, far = groups
    low_at, high_at = 0, None
    for d in range(1, last + 1):
        for g in range(2):
            if d < last:
                for way in range(2):
                    ring(way, d, g).wait_recv()
                    if d + 1 < last:
                        ring(way, d + 1, g).start()
                    else:

                        @pl.when(core == way)
                        def _():
                            ring(way, d + 1, g).start()
            else:
                ring(0, d, g).wait_recv()
        share(d, core).start()
        if d < last:
            share(nz - d, core).start()
        if d <= 2:
            for way in range(2):
                first(way, d - 1).wait_recv()
                second(way, d - 1).start()
        if d == 3:
            for r in range(2):
                for way in range(2):
                    second(way, r).wait_recv()
            scaled(1 - plane, qx)
            arrived(near[:TILE])
            first_part(near[:TILE], None, 1, 0, group)
        if d == 5:
            arrived(near[TILE:])
            first_part(near[TILE:], 1, 2, 0, group)
        if d == last - 1:
            low_at, high_at = second_part(0, 0, 2, 3, 0, group)
            arrived(middle)
            first_part(middle, high_at, high_at + 1, 0, group)
            low_at, high_at = second_part(1, low_at, high_at + 1, high_at + 2, 0, group)
    arrived(far)

    lane = lax.broadcasted_iota(jnp.int32, (tok, HEAD_SIZE), 1)
    mine = plane * heads + h
    far_first = sorted(range(1, 2 * heads), key=lambda e: (e % heads) not in (0, 2, 6))

    def spread(buffer, landing, index):
        for e in far_first:
            p, j = outward(e)
            send(
                buffer.at[p * heads + j], landing.at[mine], o_send.at[index], o_recv.at[index], device(e)
            ).start()
        pltpu.make_async_copy(buffer.at[mine], landing.at[mine], o_recv.at[index]).start()

    lse[...] = jnp.zeros_like(lse)

    def chunk_step(chunk, _):
        offset = chunk * per_chunk
        first_part(far, high_at, high_at + 1, offset, per_chunk)
        ends = second_part(2, low_at, high_at + 1, high_at + 2, offset, per_chunk)
        for side in range(2):
            for n in range(per_chunk):
                m, al = m_s[ends[side], offset + n], al_s[ends[side], offset + n]
                total = al[:, HEAD_SIZE:]
                some = total > 0.0
                safe = jnp.where(some, total, 1.0)
                mixed = (al[:, :HEAD_SIZE] / safe).astype(jnp.bfloat16)
                out_send[chunk, side * heads:(side + 1) * heads, :, n * HEAD_SIZE:(n + 1) * HEAD_SIZE] = (
                    mixed.reshape(heads, piece, HEAD_SIZE)
                )
                level = jnp.where(some, m + jnp.log2(safe), EMPTY)
                lse[side] = jnp.where(lax.rem(lane, group) == offset + n, level, lse[side])
        spread(out_send.at[chunk], out_recv.at[chunk], chunk)
        return 0

    lax.fori_loop(0, CHUNKS, chunk_step, 0)

    for side in range(2):
        level = lse[side]
        high = level.astype(jnp.bfloat16).astype(jnp.float32)
        rest = (level - high).astype(jnp.bfloat16).astype(jnp.float32)
        low = level - high - rest
        packed = jnp.where(lane < group, high, jnp.where(lane < 2 * group, rest, low)).astype(jnp.bfloat16)
        stat_send[side * heads:(side + 1) * heads] = packed.reshape(heads, piece, HEAD_SIZE)
    spread(stat_send, stat_recv, CHUNKS)

    for slot in range(nz):
        share(slot, core).wait_send()
    for g in range(2):

        @pl.when(core != plane)
        def _():
            cross_copy(g, 1 - core).wait_send()

        for d in range(1, last):
            for way in range(2):
                ring(way, d, g).wait_send()
        ring(0, last, g).wait_send()
    for r in range(2):
        for way in range(2):
            first(way, r).wait_send()
            second(way, r).wait_send()

    pltpu.make_async_copy(stat_send, stat_recv, o_recv.at[CHUNKS]).wait()
    for chunk in range(CHUNKS):
        pltpu.make_async_copy(out_send.at[chunk], out_recv.at[chunk], o_recv.at[chunk]).wait()

    for source in range(heads):
        levels = []
        for side in range(2):
            packed = stat_recv[side * heads + source].astype(jnp.float32)
            levels.append(
                packed + pltpu.roll(packed, HEAD_SIZE - group, 1) + pltpu.roll(packed, HEAD_SIZE - 2 * group, 1)
            )
        share_0 = 1.0 / (1.0 + jnp.exp2(levels[1] - levels[0]))
        for head in range(group):
            chunk, n = head // per_chunk, head % per_chunk
            columns = slice(n * HEAD_SIZE, (n + 1) * HEAD_SIZE)
            part_0 = out_recv[chunk, source, :, columns].astype(jnp.float32)
            part_1 = out_recv[chunk, heads + source, :, columns].astype(jnp.float32)
            portion = jnp.broadcast_to(share_0[:, head:head + 1], (piece, HEAD_SIZE))
            start = (source * group + head) * HEAD_SIZE
            out_ref[:, start:start + HEAD_SIZE] = (part_1 + portion * (part_0 - part_1)).astype(jnp.bfloat16)

    others = pl.ds(0, 2 * heads - 1)
    pltpu.make_async_copy(stat_send.at[others], stat_recv.at[others], o_send.at[CHUNKS]).wait()
    for chunk in range(CHUNKS):
        pltpu.make_async_copy(out_send.at[chunk, others], out_recv.at[chunk, others], o_send.at[chunk]).wait()


def solution(mesh):
    nz, heads = mesh.shape["seq"] // 4, mesh.shape["head"]
    arrival = [0] + [slot for d in range(1, nz // 2) for slot in (d, nz - d)] + [nz // 2]
    groups = (arrival[:2 * TILE], arrival[2 * TILE:3 * TILE], arrival[3 * TILE:])

    def per_device(queries, keys, values, layout):
        tok, width = queries.shape
        group = width // HEAD_SIZE
        piece = tok // heads
        entries = sum(len(slots) // TILE + 1 for slots in groups) * TILE
        states = 1 + nz // TILE + entries // TILE
        bf16, f32, dma = jnp.bfloat16, jnp.float32, pltpu.SemaphoreType.DMA
        anywhere = pl.BlockSpec(memory_space=pl.ANY)

        return pl.pallas_call(
            lambda *refs: kernel(nz, heads, groups, *refs),
            out_shape=jax.ShapeDtypeStruct((piece, heads * width), bf16),
            in_specs=[anywhere] * 4,
            out_specs=pl.BlockSpec(memory_space=pltpu.VMEM),
            scratch_shapes=[pltpu.VMEM((len(slots), 2, 2, tok, HEAD_SIZE), bf16) for slots in groups]
            + [
                pltpu.VMEM((tok, width), bf16),
                pltpu.VMEM((tok, width), bf16),
                pltpu.VMEM((2, 2, tok // 2, width // 2), bf16),
                pltpu.VMEM((2, group, tok, HEAD_SIZE), bf16),
                pltpu.VMEM((states, group, tok, HEAD_SIZE), f32),
                pltpu.VMEM((states, group, tok, 2 * HEAD_SIZE), f32),
                pltpu.VMEM((CHUNKS, 2 * heads, piece, width // CHUNKS), bf16),
                pltpu.VMEM((CHUNKS, 2 * heads, piece, width // CHUNKS), bf16),
                pltpu.VMEM((2 * heads, piece, HEAD_SIZE), bf16),
                pltpu.VMEM((2 * heads, piece, HEAD_SIZE), bf16),
                pltpu.VMEM((2, tok, HEAD_SIZE), f32),
                pltpu.SMEM(layout.shape, jnp.int32),
                pltpu.SMEM((entries,), jnp.int32),
                pltpu.SMEM((entries,), jnp.int32),
                pltpu.SMEM((3, 2 * TILE), jnp.int32),
                dma((nz, 2)), dma((nz, 2)), dma((nz,)), dma((nz,)), dma((2,)), dma((2,)),
                dma((2, 2)), dma((2, 2)), dma((2, 2)), dma((2, 2)),
                dma((CHUNKS + 1,)), dma((CHUNKS + 1,)), dma((4,)),
            ],
            compiler_params=pltpu.CompilerParams(
                collective_id=0, has_side_effects=True, vmem_limit_bytes=60 * 1024 * 1024
            ),
            cost_estimate=pl.CostEstimate(
                flops=4 * 2 * (nz + 1) * tok * group * tok * HEAD_SIZE,
                bytes_accessed=4 * tok * width,
                transcendentals=2 * (nz + 1) * tok * group * tok,
            ),
        )(layout, queries, keys, values)

    return jax.shard_map(
        per_device,
        mesh=mesh,
        in_specs=(P("seq", "head"), P("seq", "head"), P("seq", "head"), P()),
        out_specs=P(("seq", "head"), None),
        check_vma=False,
    )
```

```python
import math

import jax
import jax.numpy as jnp
from jax import lax
from jax.experimental import pallas as pl
from jax.experimental.pallas import tpu as pltpu
from jax.sharding import PartitionSpec as P


HEAD_SIZE = 128
MESH = pl.DeviceIdType.MESH
EMPTY = -1e30
SCALE = math.log2(math.e) / math.sqrt(HEAD_SIZE)
CHUNKS = 2
TILE = 4


def tiles_for(slots):
    return (len(slots) + (0 in slots) - 2) // TILE + 2


def places(nz, heads):
    seq, h = lax.axis_index("seq"), lax.axis_index("head")
    return seq // (2 * nz), (seq // 2) % nz, seq % 2, h


def send(src, dst, send_sem, recv_sem, device):
    return pltpu.make_async_remote_copy(
        src_ref=src, dst_ref=dst, send_sem=send_sem, recv_sem=recv_sem, device_id=device, device_id_type=MESH
    )


def kernel(
    nz, heads, arrival, groups, layout_hbm, q_hbm, k_ref, v_ref, out_ref,
    kv_0, kv_1, kv_2, q_ref, qx, relay, qs, m_s, al_s, out_send, out_recv, stat_send, stat_recv, lse,
    layout_ref, pick, limit, place,
    ring_send, ring_recv, share_send, share_recv, cross_send, cross_recv,
    first_send, first_recv, second_send, second_recv, o_send, o_recv, local,
):
    tok, width = q_ref.shape
    group = width // HEAD_SIZE
    per_chunk = group // CHUNKS
    piece = tok // heads
    plane, z, core, h = places(nz, heads)
    nx = heads // 2
    y_lo, x = h // nx, h % nx
    last = nz // 2

    def at(p, zz, cc):
        return (p * nz + zz) * 2 + cc

    step_to = jnp.where(core == 0, 1, nz - 1)
    onward, backward = (at(plane, (z + step_to) % nz, core), h), (at(plane, (z + nz - step_to) % nz, core), h)
    sibling = (at(plane, z, 1 - core), h)
    opposite = [(at(1 - plane, z, cc), h) for cc in range(2)]
    above = (at((plane + y_lo) % 2, z, core), (1 - y_lo) * nx + x)
    below = (at((plane + 1 - y_lo) % 2, z, core), (1 - y_lo) * nx + x)

    def outward(e):
        return (plane + e // heads) % 2, (h + e % heads) % heads

    def device(e):
        p, j = outward(e)
        return at(p, z, core), j

    buffers = (kv_0, kv_1, kv_2)

    def spot(d, whose):
        if d == 0:
            return kv_0, 0
        if d == last:
            return kv_2, len(groups[2]) - 1
        index = 2 * d - 1 + whose
        for buffer, slots, begin in zip(buffers, groups, (0, len(groups[0]), len(groups[0]) + len(groups[1]))):
            if begin <= 2 * d - 1 < begin + len(slots):
                return buffer, index - begin

    where = {slot: (buffer, n) for buffer, slots in zip(buffers, groups) for n, slot in enumerate(slots)}

    def block(slot, whose, g):
        buffer, n = where[slot]
        return buffer.at[n, whose, g]

    sides = (plane, 1 - plane)

    def granule(d, b, g):
        buffer, n = spot(d, core)
        return buffer.at[n, sides[b], g]

    def own(g):
        return pltpu.make_async_copy((k_ref, v_ref)[g], granule(0, 0, g), local.at[g])

    loads = (
        pltpu.make_async_copy(q_hbm, q_ref, local.at[2]),
        pltpu.make_async_copy(layout_hbm, layout_ref, local.at[3]),
    )

    @pl.when(core == plane)
    def _():
        for g in range(2):
            own(g).start()

    for load in loads:
        load.start()

    barrier = pltpu.get_barrier_semaphore()
    around = [onward, backward, sibling, (at(1 - plane, z, 1 - core), h)] + [device(e) for e in range(1, 2 * heads)]
    for to in around:
        pl.semaphore_signal(barrier, inc=1, device_id=to, device_id_type=MESH)
    pl.semaphore_wait(barrier, len(around))

    def ring(d, b, g):
        return send(
            granule(d - 1, b, g), granule(d, b, g), ring_send.at[d - 1, b, g], ring_recv.at[d - 1, b, g], onward
        )

    def share(d, whose):
        buffer, n = spot(d, whose)
        ref = buffer.at[n, jnp.where(whose == 0, plane, 1 - plane)] if d == last else buffer.at[n]
        return send(ref, ref, share_send.at[d - 1], share_recv.at[d - 1], sibling)

    def home(g):
        return send((k_ref, v_ref)[g], granule(0, 0, g), cross_send.at[0, g], cross_recv.at[0, g], sibling)

    def abroad(cc, g):
        return send(
            (k_ref, v_ref)[g], granule(0, 0, g), cross_send.at[cc, g], cross_recv.at[1, g], opposite[cc]
        )

    def from_abroad(g):
        return send((k_ref, v_ref)[g], granule(0, 1, g), cross_send.at[1, g], cross_recv.at[1, g], opposite[0])

    half, strip = width // 2, tok // 2

    def first(way, r):
        src = q_hbm.at[pl.ds(r * strip, strip), pl.ds(way * half, half)]
        return send(src, relay.at[way, r], first_send.at[way, r], first_recv.at[way, r], (above, below)[way])

    def second(way, r):
        dst = qx.at[pl.ds(r * strip, strip), pl.ds(way * half, half)]
        return send(relay.at[way, r], dst, second_send.at[way, r], second_recv.at[way, r], (above, below)[way])

    @pl.when(core != plane)
    def _():
        for g in range(2):
            for cc in range(2):
                abroad(cc, g).start()

    @pl.when(core == plane)
    def _():
        for g in range(2):
            home(g).start()

    for g in range(2):

        @pl.when(core != plane)
        def _():
            home(g).wait_recv()

        @pl.when(core == plane)
        def _():
            own(g).wait()

        ring(1, 0, g).start()
    for r in range(2):
        for way in range(2):
            first(way, r).start()
    for g in range(2):
        from_abroad(g).wait_recv()
        ring(1, 1, g).start()
    for load in loads:
        load.wait()

    own_block = layout_ref[2 * z + core]
    low_tiles, starts, tile_counts = [], [], []
    start = 0
    for slots in groups:
        tiles = tiles_for(slots)
        positions = [layout_ref[2 * ((z + nz - slot) % nz) + plane] for slot in slots]
        count = jnp.int32(0)
        for position in positions:
            count += (position <= own_block).astype(jnp.int32)
        low = (count + TILE - 1) // TILE
        low_next, high_next = jnp.int32(0), low * TILE
        for n, position in enumerate(positions):
            is_low, is_high = position <= own_block, position >= own_block
            place[0, n] = jnp.where(is_low, low_next, -1)
            place[1, n] = jnp.where(is_high, high_next, -1)
            place[2, n] = jnp.where(position == own_block, 0, tok)
            low_next += is_low.astype(jnp.int32)
            high_next += is_high.astype(jnp.int32)

        def order(t, _):
            index, bound = jnp.int32(0), jnp.int32(-tok)
            for n in range(len(slots)):
                here = (place[0, n] == t) | (place[1, n] == t)
                index = jnp.where(here, n, index)
                bound = jnp.where(here, place[2, n], bound)
            pick[start + t] = index
            limit[start + t] = bound
            return 0

        lax.fori_loop(0, tiles * TILE, order, 0)
        low_tiles.append(low)
        starts.append(start)
        tile_counts.append(tiles)
        start += tiles * TILE

    def scaled(target, ref):
        for head in range(group):
            part = ref[:, head * HEAD_SIZE:(head + 1) * HEAD_SIZE].astype(jnp.float32) * SCALE
            qs[target, head] = part.astype(jnp.bfloat16)

    scaled(plane, q_ref)
    ones = jnp.ones((TILE * tok, HEAD_SIZE), jnp.bfloat16)

    def tile(side, keys, values, before, after, bounds, offset, count):
        values = jnp.concatenate([values, ones], axis=1)

        def scores(n):
            return lax.dot_general(
                qs[side, offset + n], keys, (((1,), (1,)), ((), ())), preferred_element_type=jnp.float32
            )

        if bounds is not None:
            ahead = lax.broadcasted_iota(jnp.int32, (tok, tok), 1) - lax.broadcasted_iota(jnp.int32, (tok, tok), 0)
        upcoming = scores(0)
        for n in range(count):
            score = upcoming
            if n + 1 < count:
                upcoming = scores(n + 1)
            parts = [score[:, j * tok:(j + 1) * tok] for j in range(TILE)]
            if bounds is not None:
                parts = [jnp.where(ahead <= bounds[j], parts[j], EMPTY) for j in range(TILE)]
            widest = parts[0]
            for part in parts[1:]:
                widest = jnp.maximum(widest, part)
            top = jnp.max(widest, axis=1, keepdims=True)
            if before is None:
                m_next = jnp.broadcast_to(top, (tok, HEAD_SIZE))
            else:
                m = m_s[before, offset + n]
                m_next = jnp.maximum(m, top)
            weight = jnp.concatenate([jnp.exp2(part - m_next).astype(jnp.bfloat16) for part in parts], axis=1)
            mixed = jnp.dot(weight, values, preferred_element_type=jnp.float32)
            if before is not None:
                factor = jnp.exp2(m - m_next)
                mixed += al_s[before, offset + n] * jnp.concatenate([factor, factor], axis=1)
            m_s[after, offset + n] = m_next
            al_s[after, offset + n] = mixed

    m_s[0] = jnp.full(m_s.shape[1:], EMPTY, jnp.float32)
    al_s[0] = jnp.zeros(al_s.shape[1:], jnp.float32)

    def first_part(slots, before, after, offset, count):
        keys = jnp.concatenate([block(slot, 0, 0)[...] for slot in slots], axis=0)
        values = jnp.concatenate([block(slot, 0, 1)[...] for slot in slots], axis=0)
        tile(1, keys, values, before, after, None, offset, count)

    def second_part(index, low_before, high_before, after, offset, count, begin=0, end=None):
        buffer, low, base, tiles = buffers[index], low_tiles[index], starts[index], tile_counts[index]

        def step(t, _):
            side = jnp.where(t < low, 0, 1)
            before = jnp.where(t == low, high_before, jnp.where(t == 0, low_before, after + t - 1))
            chosen = [pick[base + t * TILE + j] for j in range(TILE)]
            bounds = [limit[base + t * TILE + j] for j in range(TILE)]
            keys = jnp.concatenate([buffer[n, side, 0] for n in chosen], axis=0)
            values = jnp.concatenate([buffer[n, side, 1] for n in chosen], axis=0)
            tile(side, keys, values, before, after + t, bounds, offset, count)
            return 0

        lax.fori_loop(begin, tiles if end is None else end, step, 0)
        return (
            jnp.where(low == 0, low_before, after + low - 1),
            jnp.where(low == tiles, high_before, after + tiles - 1),
        )

    def shared(*steps):
        for d in steps:
            share(d, 1 - core).wait_recv()

    parts = [arrival[i:i + TILE] for i in range(0, nz, TILE)]
    for d in range(1, last + 1):
        for b in range(2):
            if d < last - 1:
                for g in range(2):
                    ring(d, b, g).wait_recv()
                    ring(d + 1, b, g).start()
            elif d == last - 1:
                for g in range(2):
                    ring(d, b, g).wait_recv()

                @pl.when(core == b)
                def _():
                    for g in range(2):
                        ring(last, b, g).start()
            else:

                @pl.when(core == b)
                def _():
                    for g in range(2):
                        ring(last, b, g).wait_recv()
        share(d, core).start()
        if d <= 2:
            for way in range(2):
                first(way, d - 1).wait_recv()
                second(way, d - 1).start()
        if d == 3:
            for r in range(2):
                for way in range(2):
                    second(way, r).wait_recv()
            scaled(1 - plane, qx)
            shared(1, 2)
            first_part(parts[0], None, 1, 0, group)
        if d == 4:
            shared(3)
            second_part(0, 0, 1, 3, 0, group, 0, 2)
        if d == 5:
            low_at, high_at = second_part(0, 0, 1, 3, 0, group, 2, 3)
        if d == 6:
            shared(4)
            first_part(parts[1], high_at, 2, 0, group)
        if d == 7:
            shared(5, 6)
            first_part(parts[2], 2, 6, 0, group)
            low_at, high_at = second_part(1, low_at, 6, 7, 0, group)
    shared(last - 1, last)

    lane = lax.broadcasted_iota(jnp.int32, (tok, HEAD_SIZE), 1)
    mine = plane * heads + h
    far_first = sorted(range(1, 2 * heads), key=lambda e: (e % heads) not in (0, 2, 6))

    def spread(buffer, landing, index):
        for e in far_first:
            p, j = outward(e)
            send(
                buffer.at[p * heads + j], landing.at[mine], o_send.at[index], o_recv.at[index], device(e)
            ).start()
        pltpu.make_async_copy(buffer.at[mine], landing.at[mine], o_recv.at[index]).start()

    lse[...] = jnp.zeros_like(lse)

    def chunk_step(chunk, _):
        offset = chunk * per_chunk
        first_part(parts[3], high_at, 9, offset, per_chunk)
        ends = second_part(2, low_at, 9, 10, offset, per_chunk)
        for side in range(2):
            for n in range(per_chunk):
                m, al = m_s[ends[side], offset + n], al_s[ends[side], offset + n]
                total = al[:, HEAD_SIZE:]
                some = total > 0.0
                safe = jnp.where(some, total, 1.0)
                mixed = (al[:, :HEAD_SIZE] / safe).astype(jnp.bfloat16)
                out_send[chunk, side * heads:(side + 1) * heads, :, n * HEAD_SIZE:(n + 1) * HEAD_SIZE] = (
                    mixed.reshape(heads, piece, HEAD_SIZE)
                )
                level = jnp.where(some, m + jnp.log2(safe), EMPTY)
                lse[side] = jnp.where(lax.rem(lane, group) == offset + n, level, lse[side])
        spread(out_send.at[chunk], out_recv.at[chunk], chunk)
        return 0

    lax.fori_loop(0, CHUNKS, chunk_step, 0)

    for side in range(2):
        level = lse[side]
        high = level.astype(jnp.bfloat16).astype(jnp.float32)
        rest = (level - high).astype(jnp.bfloat16).astype(jnp.float32)
        low = level - high - rest
        packed = jnp.where(lane < group, high, jnp.where(lane < 2 * group, rest, low)).astype(jnp.bfloat16)
        stat_send[side * heads:(side + 1) * heads] = packed.reshape(heads, piece, HEAD_SIZE)
    spread(stat_send, stat_recv, CHUNKS)

    for d in range(1, last + 1):
        share(d, core).wait_send()
    for g in range(2):

        @pl.when(core != plane)
        def _():
            for cc in range(2):
                abroad(cc, g).wait_send()

        @pl.when(core == plane)
        def _():
            home(g).wait_send()

        for b in range(2):
            for d in range(1, last):
                ring(d, b, g).wait_send()

            @pl.when(core == b)
            def _():
                ring(last, b, g).wait_send()
    for r in range(2):
        for way in range(2):
            first(way, r).wait_send()
            second(way, r).wait_send()

    pltpu.make_async_copy(stat_send, stat_recv, o_recv.at[CHUNKS]).wait()
    for chunk in range(CHUNKS):
        pltpu.make_async_copy(out_send.at[chunk], out_recv.at[chunk], o_recv.at[chunk]).wait()

    for source in range(heads):
        levels = []
        for side in range(2):
            packed = stat_recv[side * heads + source].astype(jnp.float32)
            levels.append(
                packed + pltpu.roll(packed, HEAD_SIZE - group, 1) + pltpu.roll(packed, HEAD_SIZE - 2 * group, 1)
            )
        share_0 = 1.0 / (1.0 + jnp.exp2(levels[1] - levels[0]))
        for head in range(group):
            chunk, n = head // per_chunk, head % per_chunk
            columns = slice(n * HEAD_SIZE, (n + 1) * HEAD_SIZE)
            part_0 = out_recv[chunk, source, :, columns].astype(jnp.float32)
            part_1 = out_recv[chunk, heads + source, :, columns].astype(jnp.float32)
            portion = jnp.broadcast_to(share_0[:, head:head + 1], (piece, HEAD_SIZE))
            start = (source * group + head) * HEAD_SIZE
            out_ref[:, start:start + HEAD_SIZE] = (part_1 + portion * (part_0 - part_1)).astype(jnp.bfloat16)

    others = pl.ds(0, 2 * heads - 1)
    pltpu.make_async_copy(stat_send.at[others], stat_recv.at[others], o_send.at[CHUNKS]).wait()
    for chunk in range(CHUNKS):
        pltpu.make_async_copy(out_send.at[chunk, others], out_recv.at[chunk, others], o_send.at[chunk]).wait()


def solution(mesh):
    nz, heads = mesh.shape["seq"] // 4, mesh.shape["head"]
    arrival = [0] + [slot for d in range(1, nz // 2) for slot in (d, nz - d)] + [nz // 2]
    groups = (arrival[:2 * TILE - 1], arrival[2 * TILE - 1:3 * TILE - 1], arrival[3 * TILE - 1:])

    def per_device(queries, keys, values, layout):
        tok, width = queries.shape
        group = width // HEAD_SIZE
        piece = tok // heads
        entries = sum(tiles_for(slots) for slots in groups) * TILE
        states = 1 + nz // TILE + entries // TILE
        bf16, f32, dma = jnp.bfloat16, jnp.float32, pltpu.SemaphoreType.DMA
        anywhere = pl.BlockSpec(memory_space=pl.ANY)

        return pl.pallas_call(
            lambda *refs: kernel(nz, heads, arrival, groups, *refs),
            out_shape=jax.ShapeDtypeStruct((piece, heads * width), bf16),
            in_specs=[anywhere] * 4,
            out_specs=pl.BlockSpec(memory_space=pltpu.VMEM),
            scratch_shapes=[pltpu.VMEM((len(slots), 2, 2, tok, HEAD_SIZE), bf16) for slots in groups]
            + [
                pltpu.VMEM((tok, width), bf16),
                pltpu.VMEM((tok, width), bf16),
                pltpu.VMEM((2, 2, tok // 2, width // 2), bf16),
                pltpu.VMEM((2, group, tok, HEAD_SIZE), bf16),
                pltpu.VMEM((states, group, tok, HEAD_SIZE), f32),
                pltpu.VMEM((states, group, tok, 2 * HEAD_SIZE), f32),
                pltpu.VMEM((CHUNKS, 2 * heads, piece, width // CHUNKS), bf16),
                pltpu.VMEM((CHUNKS, 2 * heads, piece, width // CHUNKS), bf16),
                pltpu.VMEM((2 * heads, piece, HEAD_SIZE), bf16),
                pltpu.VMEM((2 * heads, piece, HEAD_SIZE), bf16),
                pltpu.VMEM((2, tok, HEAD_SIZE), f32),
                pltpu.SMEM(layout.shape, jnp.int32),
                pltpu.SMEM((entries,), jnp.int32),
                pltpu.SMEM((entries,), jnp.int32),
                pltpu.SMEM((3, 2 * TILE), jnp.int32),
                dma((nz // 2, 2, 2)), dma((nz // 2, 2, 2)), dma((nz // 2,)), dma((nz // 2,)), dma((2, 2)), dma((2, 2)),
                dma((2, 2)), dma((2, 2)), dma((2, 2)), dma((2, 2)),
                dma((CHUNKS + 1,)), dma((CHUNKS + 1,)), dma((4,)),
            ],
            compiler_params=pltpu.CompilerParams(
                collective_id=0, has_side_effects=True, vmem_limit_bytes=60 * 1024 * 1024
            ),
            cost_estimate=pl.CostEstimate(
                flops=4 * 2 * (nz + 1) * tok * group * tok * HEAD_SIZE,
                bytes_accessed=4 * tok * width,
                transcendentals=2 * (nz + 1) * tok * group * tok,
            ),
        )(layout, queries, keys, values)

    return jax.shard_map(
        per_device,
        mesh=mesh,
        in_specs=(P("seq", "head"), P("seq", "head"), P("seq", "head"), P()),
        out_specs=P(("seq", "head"), None),
        check_vma=False,
    )
```

```python
import math

import jax
import jax.numpy as jnp
from jax import lax
from jax.experimental import pallas as pl
from jax.experimental.pallas import tpu as pltpu
from jax.sharding import PartitionSpec as P


HEAD_SIZE = 128
MESH = pl.DeviceIdType.MESH
EMPTY = -1e30
SCALE = math.log2(math.e) / math.sqrt(HEAD_SIZE)
CHUNKS = 2
TILE = 4


def tiles_for(slots):
    return (len(slots) + (0 in slots) - 2) // TILE + 2


def places(nz, heads):
    seq, h = lax.axis_index("seq"), lax.axis_index("head")
    return seq // (2 * nz), (seq // 2) % nz, seq % 2, h


def send(src, dst, send_sem, recv_sem, device):
    return pltpu.make_async_remote_copy(
        src_ref=src, dst_ref=dst, send_sem=send_sem, recv_sem=recv_sem, device_id=device, device_id_type=MESH
    )


def kernel(
    nz, heads, arrival, groups, layout_hbm, q_hbm, k_ref, v_ref, out_ref,
    kv_0, kv_1, kv_2, q_ref, qx, relay, qs, m_s, al_s, out_send, out_recv, stat_send, stat_recv, lse,
    layout_ref, pick, limit, place,
    ring_send, ring_recv, share_send, share_recv, cross_send, cross_recv,
    first_send, first_recv, second_send, second_recv, o_send, o_recv, local,
):
    tok, width = q_ref.shape
    group = width // HEAD_SIZE
    per_chunk = group // CHUNKS
    piece = tok // heads
    plane, z, core, h = places(nz, heads)
    nx = heads // 2
    y_lo, x = h // nx, h % nx
    last = nz // 2

    def at(p, zz, cc):
        return (p * nz + zz) * 2 + cc

    step_to = jnp.where(core == 0, 1, nz - 1)
    onward, backward = (at(plane, (z + step_to) % nz, core), h), (at(plane, (z + nz - step_to) % nz, core), h)
    sibling = (at(plane, z, 1 - core), h)
    opposite = [(at(1 - plane, z, cc), h) for cc in range(2)]
    above = (at((plane + y_lo) % 2, z, core), (1 - y_lo) * nx + x)
    below = (at((plane + 1 - y_lo) % 2, z, core), (1 - y_lo) * nx + x)

    def outward(e):
        return (plane + e // heads) % 2, (h + e % heads) % heads

    def device(e):
        p, j = outward(e)
        return at(p, z, core), j

    buffers = (kv_0, kv_1, kv_2)

    def spot(d, whose):
        if d == 0:
            return kv_0, 0
        if d == last:
            return kv_2, len(groups[2]) - 1
        index = 2 * d - 1 + whose
        for buffer, slots, begin in zip(buffers, groups, (0, len(groups[0]), len(groups[0]) + len(groups[1]))):
            if begin <= 2 * d - 1 < begin + len(slots):
                return buffer, index - begin

    where = {slot: (buffer, n) for buffer, slots in zip(buffers, groups) for n, slot in enumerate(slots)}

    def block(slot, whose, g):
        buffer, n = where[slot]
        return buffer.at[n, whose, g]

    sides = (plane, 1 - plane)

    def granule(d, b, g):
        buffer, n = spot(d, core)
        return buffer.at[n, sides[b], g]

    def own(g):
        return pltpu.make_async_copy((k_ref, v_ref)[g], granule(0, 0, g), local.at[g])

    loads = (
        pltpu.make_async_copy(q_hbm, q_ref, local.at[2]),
        pltpu.make_async_copy(layout_hbm, layout_ref, local.at[3]),
    )

    @pl.when(core == plane)
    def _():
        for g in range(2):
            own(g).start()

    for load in loads:
        load.start()

    barrier = pltpu.get_barrier_semaphore()
    around = [onward, backward, sibling, (at(1 - plane, z, 1 - core), h)] + [device(e) for e in range(1, 2 * heads)]
    for to in around:
        pl.semaphore_signal(barrier, inc=1, device_id=to, device_id_type=MESH)
    pl.semaphore_wait(barrier, len(around))

    def ring(d, b, g):
        return send(
            granule(d - 1, b, g), granule(d, b, g), ring_send.at[d - 1, b, g], ring_recv.at[d - 1, b, g], onward
        )

    def share(d, whose):
        buffer, n = spot(d, whose)
        ref = buffer.at[n, jnp.where(whose == 0, plane, 1 - plane)] if d == last else buffer.at[n]
        return send(ref, ref, share_send.at[d - 1], share_recv.at[d - 1], sibling)

    def home(g):
        return send((k_ref, v_ref)[g], granule(0, 0, g), cross_send.at[0, g], cross_recv.at[0, g], sibling)

    def abroad(cc, g):
        return send(
            (k_ref, v_ref)[g], granule(0, 0, g), cross_send.at[cc, g], cross_recv.at[1, g], opposite[cc]
        )

    def from_abroad(g):
        return send((k_ref, v_ref)[g], granule(0, 1, g), cross_send.at[1, g], cross_recv.at[1, g], opposite[0])

    half, strip = width // 2, tok // 2

    def first(way, r):
        src = q_hbm.at[pl.ds(r * strip, strip), pl.ds(way * half, half)]
        return send(src, relay.at[way, r], first_send.at[way, r], first_recv.at[way, r], (above, below)[way])

    def second(way, r):
        dst = qx.at[pl.ds(r * strip, strip), pl.ds(way * half, half)]
        return send(relay.at[way, r], dst, second_send.at[way, r], second_recv.at[way, r], (above, below)[way])

    @pl.when(core != plane)
    def _():
        for g in range(2):
            for cc in range(2):
                abroad(cc, g).start()

    @pl.when(core == plane)
    def _():
        for g in range(2):
            home(g).start()

    for g in range(2):

        @pl.when(core != plane)
        def _():
            home(g).wait_recv()

        @pl.when(core == plane)
        def _():
            own(g).wait()

        ring(1, 0, g).start()
    for r in range(2):
        for way in range(2):
            first(way, r).start()
    for g in range(2):
        from_abroad(g).wait_recv()
        ring(1, 1, g).start()

    own_block, low_tiles, starts, tile_counts = [], [], [], []

    def arrange(slots):
        tiles, start = tiles_for(slots), sum(tile_counts) * TILE
        positions = [layout_ref[2 * ((z + nz - slot) % nz) + plane] for slot in slots]
        count = jnp.int32(0)
        for position in positions:
            count += (position <= own_block[0]).astype(jnp.int32)
        low = (count + TILE - 1) // TILE
        low_next, high_next = jnp.int32(0), low * TILE
        for n, position in enumerate(positions):
            is_low, is_high = position <= own_block[0], position >= own_block[0]
            place[0, n] = jnp.where(is_low, low_next, -1)
            place[1, n] = jnp.where(is_high, high_next, -1)
            place[2, n] = jnp.where(position == own_block[0], 0, tok)
            low_next += is_low.astype(jnp.int32)
            high_next += is_high.astype(jnp.int32)

        def order(t, _):
            index, bound = jnp.int32(0), jnp.int32(-tok)
            for n in range(len(slots)):
                here = (place[0, n] == t) | (place[1, n] == t)
                index = jnp.where(here, n, index)
                bound = jnp.where(here, place[2, n], bound)
            pick[start + t] = index
            limit[start + t] = bound
            return 0

        lax.fori_loop(0, tiles * TILE, order, 0)
        low_tiles.append(low)
        starts.append(start)
        tile_counts.append(tiles)

    def scaled(target, ref):
        for head in range(group):
            part = ref[:, head * HEAD_SIZE:(head + 1) * HEAD_SIZE].astype(jnp.float32) * SCALE
            qs[target, head] = part.astype(jnp.bfloat16)

    ones = jnp.ones((TILE * tok, HEAD_SIZE), jnp.bfloat16)

    def tile(side, keys, values, before, after, bounds, offset, count):
        values = jnp.concatenate([values, ones], axis=1)

        def scores(n):
            return lax.dot_general(
                qs[side, offset + n], keys, (((1,), (1,)), ((), ())), preferred_element_type=jnp.float32
            )

        if bounds is not None:
            ahead = lax.broadcasted_iota(jnp.int32, (tok, tok), 1) - lax.broadcasted_iota(jnp.int32, (tok, tok), 0)
        upcoming = scores(0)
        for n in range(count):
            score = upcoming
            if n + 1 < count:
                upcoming = scores(n + 1)
            parts = [score[:, j * tok:(j + 1) * tok] for j in range(TILE)]
            if bounds is not None:
                parts = [jnp.where(ahead <= bounds[j], parts[j], EMPTY) for j in range(TILE)]
            widest = parts[0]
            for part in parts[1:]:
                widest = jnp.maximum(widest, part)
            top = jnp.max(widest, axis=1, keepdims=True)
            if before is None:
                m_next = jnp.broadcast_to(top, (tok, HEAD_SIZE))
            else:
                m = m_s[before, offset + n]
                m_next = jnp.maximum(m, top)
            weight = jnp.concatenate([jnp.exp2(part - m_next).astype(jnp.bfloat16) for part in parts], axis=1)
            mixed = jnp.dot(weight, values, preferred_element_type=jnp.float32)
            if before is not None:
                factor = jnp.exp2(m - m_next)
                mixed += al_s[before, offset + n] * jnp.concatenate([factor, factor], axis=1)
            m_s[after, offset + n] = m_next
            al_s[after, offset + n] = mixed

    def first_part(slots, before, after, offset, count):
        keys = jnp.concatenate([block(slot, 0, 0)[...] for slot in slots], axis=0)
        values = jnp.concatenate([block(slot, 0, 1)[...] for slot in slots], axis=0)
        tile(1, keys, values, before, after, None, offset, count)

    def second_part(index, low_before, high_before, after, offset, count, begin=0, end=None):
        buffer, low, base, tiles = buffers[index], low_tiles[index], starts[index], tile_counts[index]

        def step(t, _):
            side = jnp.where(t < low, 0, 1)
            before = jnp.where(t == low, high_before, jnp.where(t == 0, low_before, after + t - 1))
            chosen = [pick[base + t * TILE + j] for j in range(TILE)]
            bounds = [limit[base + t * TILE + j] for j in range(TILE)]
            keys = jnp.concatenate([buffer[n, side, 0] for n in chosen], axis=0)
            values = jnp.concatenate([buffer[n, side, 1] for n in chosen], axis=0)
            tile(side, keys, values, before, after + t, bounds, offset, count)
            return 0

        if end is None:
            lax.fori_loop(0, tiles, step, 0)
        else:
            for t in range(begin, end):
                step(t, 0)
        return (
            jnp.where(low == 0, low_before, after + low - 1),
            jnp.where(low == tiles, high_before, after + tiles - 1),
        )

    def shared(*steps):
        for d in steps:
            share(d, 1 - core).wait_recv()

    parts = [arrival[i:i + TILE] for i in range(0, nz, TILE)]
    ends = {}

    def lists(index):
        if index == 0:
            loads[1].wait()
            own_block.append(layout_ref[2 * z + core])
        arrange(groups[index])

    def scale_own():
        loads[0].wait()
        scaled(plane, q_ref)

    def empty_state():
        m_s[0] = jnp.full(m_s.shape[1:], EMPTY, jnp.float32)
        al_s[0] = jnp.zeros(al_s.shape[1:], jnp.float32)

    def relay_on(r):
        for way in range(2):
            first(way, r).wait_recv()
            second(way, r).start()

    def scale_other():
        for r in range(2):
            for way in range(2):
                second(way, r).wait_recv()
        scaled(1 - plane, qx)

    def upper(index, before, after, chunk):
        first_part(parts[index], before() if callable(before) else before, after, chunk * per_chunk, per_chunk)

    def picked(index, low_before, high_before, after, t, chunk):
        low_before = low_before() if callable(low_before) else low_before
        ends[index] = second_part(
            index, low_before, high_before, after, chunk * per_chunk, per_chunk, t, t + 1
        )

    def near_low():
        return ends[0][0]

    def near_high():
        return ends[0][1]

    def lower_of(t, chunk):
        return lambda: picked(1, near_low, 2, 7, t, chunk)

    def near_of(t, chunk):
        return lambda: picked(0, 0, 1, 3, t, chunk)

    work = {
        (1, 1): [scale_own],
        (1, 2): [lambda: lists(0)],
        (1, 3): [lambda: relay_on(0)],
        (2, 1): [lambda: lists(1), lambda: lists(2)],
        (2, 2): [empty_state],
        (2, 3): [lambda: relay_on(1)],
        (3, 2): [scale_other],
        (3, 3): [lambda: shared(1, 2), lambda: upper(0, None, 1, 0)],
        (4, 1): [lambda: upper(0, None, 1, 1)],
        (4, 2): [lambda: shared(3), near_of(0, 0)],
        (4, 3): [near_of(0, 1)],
        (5, 1): [near_of(1, 0)],
        (5, 2): [near_of(1, 1)],
        (5, 3): [near_of(2, 0)],
        (6, 1): [near_of(2, 1)],
        (6, 2): [lambda: shared(4), lambda: upper(1, near_high, 2, 0)],
        (6, 3): [lambda: upper(1, near_high, 2, 1)],
        (7, 1): [lambda: shared(5), lower_of(0, 0)],
        (7, 2): [lower_of(0, 1)],
        (7, 3): [
            lower_of(1, 0), lower_of(1, 1), lambda: shared(6),
            lambda: upper(2, lambda: ends[1][1], 6, 0), lambda: upper(2, lambda: ends[1][1], 6, 1),
        ],
    }

    for d in range(1, last + 1):
        for b in range(2):
            for g in range(2):
                if d < last:
                    ring(d, b, g).wait_recv()
                    if d + 1 < last:
                        ring(d + 1, b, g).start()
                    else:

                        @pl.when(core == b)
                        def _():
                            ring(last, b, g).start()
                else:

                    @pl.when(core == b)
                    def _():
                        ring(last, b, g).wait_recv()
                if (b, g) == (1, 1):
                    share(d, core).start()
                for task in work.get((d, 2 * b + g), ()):
                    task()
    low_at, high_at = ends[1][0], 6
    shared(last - 1, last)

    lane = lax.broadcasted_iota(jnp.int32, (tok, HEAD_SIZE), 1)
    mine = plane * heads + h
    far_first = sorted(range(1, 2 * heads), key=lambda e: (e % heads) not in (0, 2, 6))

    def spread(buffer, landing, index):
        for e in far_first:
            p, j = outward(e)
            send(
                buffer.at[p * heads + j], landing.at[mine], o_send.at[index], o_recv.at[index], device(e)
            ).start()
        pltpu.make_async_copy(buffer.at[mine], landing.at[mine], o_recv.at[index]).start()

    lse[...] = jnp.zeros_like(lse)

    def chunk_step(chunk, _):
        offset = chunk * per_chunk
        first_part(parts[3], high_at, 9, offset, per_chunk)
        ends = second_part(2, low_at, 9, 10, offset, per_chunk)
        for side in range(2):
            for n in range(per_chunk):
                m, al = m_s[ends[side], offset + n], al_s[ends[side], offset + n]
                total = al[:, HEAD_SIZE:]
                some = total > 0.0
                safe = jnp.where(some, total, 1.0)
                mixed = (al[:, :HEAD_SIZE] / safe).astype(jnp.bfloat16)
                out_send[chunk, side * heads:(side + 1) * heads, :, n * HEAD_SIZE:(n + 1) * HEAD_SIZE] = (
                    mixed.reshape(heads, piece, HEAD_SIZE)
                )
                level = jnp.where(some, m + jnp.log2(safe), EMPTY)
                lse[side] = jnp.where(lax.rem(lane, group) == offset + n, level, lse[side])
        spread(out_send.at[chunk], out_recv.at[chunk], chunk)
        return 0

    lax.fori_loop(0, CHUNKS, chunk_step, 0)

    for side in range(2):
        level = lse[side]
        high = level.astype(jnp.bfloat16).astype(jnp.float32)
        rest = (level - high).astype(jnp.bfloat16).astype(jnp.float32)
        low = level - high - rest
        packed = jnp.where(lane < group, high, jnp.where(lane < 2 * group, rest, low)).astype(jnp.bfloat16)
        stat_send[side * heads:(side + 1) * heads] = packed.reshape(heads, piece, HEAD_SIZE)
    spread(stat_send, stat_recv, CHUNKS)

    for d in range(1, last + 1):
        share(d, core).wait_send()
    for g in range(2):

        @pl.when(core != plane)
        def _():
            for cc in range(2):
                abroad(cc, g).wait_send()

        @pl.when(core == plane)
        def _():
            home(g).wait_send()

        for b in range(2):
            for d in range(1, last):
                ring(d, b, g).wait_send()

            @pl.when(core == b)
            def _():
                ring(last, b, g).wait_send()
    for r in range(2):
        for way in range(2):
            first(way, r).wait_send()
            second(way, r).wait_send()

    pltpu.make_async_copy(stat_send, stat_recv, o_recv.at[CHUNKS]).wait()
    for chunk in range(CHUNKS):
        pltpu.make_async_copy(out_send.at[chunk], out_recv.at[chunk], o_recv.at[chunk]).wait()

    for source in range(heads):
        levels = []
        for side in range(2):
            packed = stat_recv[side * heads + source].astype(jnp.float32)
            levels.append(
                packed + pltpu.roll(packed, HEAD_SIZE - group, 1) + pltpu.roll(packed, HEAD_SIZE - 2 * group, 1)
            )
        share_0 = 1.0 / (1.0 + jnp.exp2(levels[1] - levels[0]))
        for head in range(group):
            chunk, n = head // per_chunk, head % per_chunk
            columns = slice(n * HEAD_SIZE, (n + 1) * HEAD_SIZE)
            part_0 = out_recv[chunk, source, :, columns].astype(jnp.float32)
            part_1 = out_recv[chunk, heads + source, :, columns].astype(jnp.float32)
            portion = jnp.broadcast_to(share_0[:, head:head + 1], (piece, HEAD_SIZE))
            start = (source * group + head) * HEAD_SIZE
            out_ref[:, start:start + HEAD_SIZE] = (part_1 + portion * (part_0 - part_1)).astype(jnp.bfloat16)

    others = pl.ds(0, 2 * heads - 1)
    pltpu.make_async_copy(stat_send.at[others], stat_recv.at[others], o_send.at[CHUNKS]).wait()
    for chunk in range(CHUNKS):
        pltpu.make_async_copy(out_send.at[chunk, others], out_recv.at[chunk, others], o_send.at[chunk]).wait()


def solution(mesh):
    nz, heads = mesh.shape["seq"] // 4, mesh.shape["head"]
    arrival = [0] + [slot for d in range(1, nz // 2) for slot in (d, nz - d)] + [nz // 2]
    groups = (arrival[:2 * TILE - 1], arrival[2 * TILE - 1:3 * TILE - 1], arrival[3 * TILE - 1:])

    def per_device(queries, keys, values, layout):
        tok, width = queries.shape
        group = width // HEAD_SIZE
        piece = tok // heads
        entries = sum(tiles_for(slots) for slots in groups) * TILE
        states = 1 + nz // TILE + entries // TILE
        bf16, f32, dma = jnp.bfloat16, jnp.float32, pltpu.SemaphoreType.DMA
        anywhere = pl.BlockSpec(memory_space=pl.ANY)

        return pl.pallas_call(
            lambda *refs: kernel(nz, heads, arrival, groups, *refs),
            out_shape=jax.ShapeDtypeStruct((piece, heads * width), bf16),
            in_specs=[anywhere] * 4,
            out_specs=pl.BlockSpec(memory_space=pltpu.VMEM),
            scratch_shapes=[pltpu.VMEM((len(slots), 2, 2, tok, HEAD_SIZE), bf16) for slots in groups]
            + [
                pltpu.VMEM((tok, width), bf16),
                pltpu.VMEM((tok, width), bf16),
                pltpu.VMEM((2, 2, tok // 2, width // 2), bf16),
                pltpu.VMEM((2, group, tok, HEAD_SIZE), bf16),
                pltpu.VMEM((states, group, tok, HEAD_SIZE), f32),
                pltpu.VMEM((states, group, tok, 2 * HEAD_SIZE), f32),
                pltpu.VMEM((CHUNKS, 2 * heads, piece, width // CHUNKS), bf16),
                pltpu.VMEM((CHUNKS, 2 * heads, piece, width // CHUNKS), bf16),
                pltpu.VMEM((2 * heads, piece, HEAD_SIZE), bf16),
                pltpu.VMEM((2 * heads, piece, HEAD_SIZE), bf16),
                pltpu.VMEM((2, tok, HEAD_SIZE), f32),
                pltpu.SMEM(layout.shape, jnp.int32),
                pltpu.SMEM((entries,), jnp.int32),
                pltpu.SMEM((entries,), jnp.int32),
                pltpu.SMEM((3, 2 * TILE), jnp.int32),
                dma((nz // 2, 2, 2)), dma((nz // 2, 2, 2)), dma((nz // 2,)), dma((nz // 2,)), dma((2, 2)), dma((2, 2)),
                dma((2, 2)), dma((2, 2)), dma((2, 2)), dma((2, 2)),
                dma((CHUNKS + 1,)), dma((CHUNKS + 1,)), dma((4,)),
            ],
            compiler_params=pltpu.CompilerParams(
                collective_id=0, has_side_effects=True, vmem_limit_bytes=60 * 1024 * 1024
            ),
            cost_estimate=pl.CostEstimate(
                flops=4 * 2 * (nz + 1) * tok * group * tok * HEAD_SIZE,
                bytes_accessed=4 * tok * width,
                transcendentals=2 * (nz + 1) * tok * group * tok,
            ),
        )(layout, queries, keys, values)

    return jax.shard_map(
        per_device,
        mesh=mesh,
        in_specs=(P("seq", "head"), P("seq", "head"), P("seq", "head"), P()),
        out_specs=P(("seq", "head"), None),
        check_vma=False,
    )
```

```python
import math

import jax
import jax.numpy as jnp
from jax import lax
from jax.experimental import pallas as pl
from jax.experimental.pallas import tpu as pltpu
from jax.sharding import PartitionSpec as P


HEAD_SIZE = 128
MESH = pl.DeviceIdType.MESH
EMPTY = -1e30
SCALE = math.log2(math.e) / math.sqrt(HEAD_SIZE)
CHUNKS = 2
TILE = 4


def tiles_for(slots):
    return (len(slots) + (0 in slots) - 2) // TILE + 2


def places(nz, heads):
    seq, h = lax.axis_index("seq"), lax.axis_index("head")
    return seq // (2 * nz), (seq // 2) % nz, seq % 2, h


def send(src, dst, send_sem, recv_sem, device):
    return pltpu.make_async_remote_copy(
        src_ref=src, dst_ref=dst, send_sem=send_sem, recv_sem=recv_sem, device_id=device, device_id_type=MESH
    )


def kernel(
    nz, heads, arrival, groups, layout_hbm, q_hbm, k_ref, v_ref, out_ref,
    kv_0, kv_1, kv_2, q_ref, qx, relay, qs, m_s, al_s, out_send, out_recv, stat_send, stat_recv, lse,
    layout_ref, pick, limit, place,
    ring_send, ring_recv, share_send, share_recv, cross_send, cross_recv,
    first_send, first_recv, second_send, second_recv, o_send, o_recv, local,
):
    tok, width = q_ref.shape
    group = width // HEAD_SIZE
    per_chunk = group // CHUNKS
    piece = tok // heads
    plane, z, core, h = places(nz, heads)
    nx = heads // 2
    y_lo, x = h // nx, h % nx
    last = nz // 2

    def at(p, zz, cc):
        return (p * nz + zz) * 2 + cc

    step_to = jnp.where(core == 0, 1, nz - 1)
    onward, backward = (at(plane, (z + step_to) % nz, core), h), (at(plane, (z + nz - step_to) % nz, core), h)
    sibling = (at(plane, z, 1 - core), h)
    opposite = [(at(1 - plane, z, cc), h) for cc in range(2)]
    above = (at((plane + y_lo) % 2, z, core), (1 - y_lo) * nx + x)
    below = (at((plane + 1 - y_lo) % 2, z, core), (1 - y_lo) * nx + x)

    def outward(e):
        return (plane + e // heads) % 2, (h + e % heads) % heads

    def device(e):
        p, j = outward(e)
        return at(p, z, core), j

    buffers = (kv_0, kv_1, kv_2)

    def spot(d, whose):
        if d == 0:
            return kv_0, 0
        if d == last:
            return kv_2, len(groups[2]) - 1
        index = 2 * d - 1 + whose
        for buffer, slots, begin in zip(buffers, groups, (0, len(groups[0]), len(groups[0]) + len(groups[1]))):
            if begin <= 2 * d - 1 < begin + len(slots):
                return buffer, index - begin

    where = {slot: (buffer, n) for buffer, slots in zip(buffers, groups) for n, slot in enumerate(slots)}

    def block(slot, whose, g):
        buffer, n = where[slot]
        return buffer.at[n, whose, g]

    sides = (plane, 1 - plane)

    def granule(d, b, g):
        buffer, n = spot(d, core)
        return buffer.at[n, sides[b], g if b == 0 else (core + g) % 2]

    def own(g):
        return pltpu.make_async_copy((k_ref, v_ref)[g], granule(0, 0, g), local.at[g])

    loads = (
        pltpu.make_async_copy(q_hbm, q_ref, local.at[2]),
        pltpu.make_async_copy(layout_hbm, layout_ref, local.at[3]),
    )

    @pl.when(core == plane)
    def _():
        for g in range(2):
            own(g).start()

    for load in loads:
        load.start()

    barrier = pltpu.get_barrier_semaphore()
    around = [onward, backward, sibling, (at(1 - plane, z, 1 - core), h)] + [device(e) for e in range(1, 2 * heads)]
    for to in around:
        pl.semaphore_signal(barrier, inc=1, device_id=to, device_id_type=MESH)
    pl.semaphore_wait(barrier, len(around))

    def ring(d, b, g):
        return send(
            granule(d - 1, b, g), granule(d, b, g), ring_send.at[d - 1, b, g], ring_recv.at[d - 1, b, g], onward
        )

    def share(d, whose):
        buffer, n = spot(d, whose)
        ref = buffer.at[n, jnp.where(whose == 0, plane, 1 - plane)] if d == last else buffer.at[n]
        return send(ref, ref, share_send.at[d - 1], share_recv.at[d - 1], sibling)

    def home(g):
        return send((k_ref, v_ref)[g], granule(0, 0, g), cross_send.at[0, g], cross_recv.at[0, g], sibling)

    def abroad(g):
        return send((k_ref, v_ref)[g], kv_0.at[0, plane, g], cross_send.at[0, g], cross_recv.at[1, 0], opposite[g])

    def pass_on():
        return send(granule(0, 1, 0), granule(0, 1, 0), cross_send.at[1, 0], cross_recv.at[1, 1], sibling)

    def passed():
        return send(granule(0, 1, 1), granule(0, 1, 1), cross_send.at[1, 0], cross_recv.at[1, 1], sibling)

    half, strip = width // 2, tok // 2

    def first(way, r):
        src = q_hbm.at[pl.ds(r * strip, strip), pl.ds(way * half, half)]
        return send(src, relay.at[way, r], first_send.at[way, r], first_recv.at[way, r], (above, below)[way])

    def second(way, r):
        dst = qx.at[pl.ds(r * strip, strip), pl.ds(way * half, half)]
        return send(relay.at[way, r], dst, second_send.at[way, r], second_recv.at[way, r], (above, below)[way])

    @pl.when(core != plane)
    def _():
        for g in range(2):
            abroad(g).start()

    @pl.when(core == plane)
    def _():
        for g in range(2):
            home(g).start()

    for g in range(2):

        @pl.when(core != plane)
        def _():
            home(g).wait_recv()

        @pl.when(core == plane)
        def _():
            own(g).wait()

        ring(1, 0, g).start()
    send(k_ref, granule(0, 1, 0), cross_send.at[0, 0], cross_recv.at[1, 0], opposite[0]).wait_recv()
    ring(1, 1, 0).start()
    pass_on().start()
    for r in range(2):
        for way in range(2):
            first(way, r).start()
    passed().wait_recv()
    ring(1, 1, 1).start()

    own_block, low_tiles, starts, tile_counts = [], [], [], []

    def arrange(slots):
        tiles, start = tiles_for(slots), sum(tile_counts) * TILE
        positions = [layout_ref[2 * ((z + nz - slot) % nz) + plane] for slot in slots]
        count = jnp.int32(0)
        for position in positions:
            count += (position <= own_block[0]).astype(jnp.int32)
        low = (count + TILE - 1) // TILE
        low_next, high_next = jnp.int32(0), low * TILE
        for n, position in enumerate(positions):
            is_low, is_high = position <= own_block[0], position >= own_block[0]
            place[0, n] = jnp.where(is_low, low_next, -1)
            place[1, n] = jnp.where(is_high, high_next, -1)
            place[2, n] = jnp.where(position == own_block[0], 0, tok)
            low_next += is_low.astype(jnp.int32)
            high_next += is_high.astype(jnp.int32)

        def order(t, _):
            index, bound = jnp.int32(0), jnp.int32(-tok)
            for n in range(len(slots)):
                here = (place[0, n] == t) | (place[1, n] == t)
                index = jnp.where(here, n, index)
                bound = jnp.where(here, place[2, n], bound)
            pick[start + t] = index
            limit[start + t] = bound
            return 0

        lax.fori_loop(0, tiles * TILE, order, 0)
        low_tiles.append(low)
        starts.append(start)
        tile_counts.append(tiles)

    def scaled(target, ref):
        for head in range(group):
            part = ref[:, head * HEAD_SIZE:(head + 1) * HEAD_SIZE].astype(jnp.float32) * SCALE
            qs[target, head] = part.astype(jnp.bfloat16)

    ones = jnp.ones((TILE * tok, HEAD_SIZE), jnp.bfloat16)

    def tile(side, keys, values, before, after, bounds, offset, count):
        values = jnp.concatenate([values, ones], axis=1)

        def scores(n):
            return lax.dot_general(
                qs[side, offset + n], keys, (((1,), (1,)), ((), ())), preferred_element_type=jnp.float32
            )

        if bounds is not None:
            ahead = lax.broadcasted_iota(jnp.int32, (tok, tok), 1) - lax.broadcasted_iota(jnp.int32, (tok, tok), 0)
        upcoming = scores(0)
        for n in range(count):
            score = upcoming
            if n + 1 < count:
                upcoming = scores(n + 1)
            parts = [score[:, j * tok:(j + 1) * tok] for j in range(TILE)]
            if bounds is not None:
                parts = [jnp.where(ahead <= bounds[j], parts[j], EMPTY) for j in range(TILE)]
            widest = parts[0]
            for part in parts[1:]:
                widest = jnp.maximum(widest, part)
            top = jnp.max(widest, axis=1, keepdims=True)
            if before is None:
                m_next = jnp.broadcast_to(top, (tok, HEAD_SIZE))
            else:
                m = m_s[before, offset + n]
                m_next = jnp.maximum(m, top)
            weight = jnp.concatenate([jnp.exp2(part - m_next).astype(jnp.bfloat16) for part in parts], axis=1)
            mixed = jnp.dot(weight, values, preferred_element_type=jnp.float32)
            if before is not None:
                factor = jnp.exp2(m - m_next)
                mixed += al_s[before, offset + n] * jnp.concatenate([factor, factor], axis=1)
            m_s[after, offset + n] = m_next
            al_s[after, offset + n] = mixed

    def first_part(slots, before, after, offset, count):
        keys = jnp.concatenate([block(slot, 0, 0)[...] for slot in slots], axis=0)
        values = jnp.concatenate([block(slot, 0, 1)[...] for slot in slots], axis=0)
        tile(1, keys, values, before, after, None, offset, count)

    def second_part(index, low_before, high_before, after, offset, count, begin=0, end=None):
        buffer, low, base, tiles = buffers[index], low_tiles[index], starts[index], tile_counts[index]

        def step(t, _):
            side = jnp.where(t < low, 0, 1)
            before = jnp.where(t == low, high_before, jnp.where(t == 0, low_before, after + t - 1))
            chosen = [pick[base + t * TILE + j] for j in range(TILE)]
            bounds = [limit[base + t * TILE + j] for j in range(TILE)]
            keys = jnp.concatenate([buffer[n, side, 0] for n in chosen], axis=0)
            values = jnp.concatenate([buffer[n, side, 1] for n in chosen], axis=0)
            tile(side, keys, values, before, after + t, bounds, offset, count)
            return 0

        lax.fori_loop(begin, tiles if end is None else end, step, 0)
        return (
            jnp.where(low == 0, low_before, after + low - 1),
            jnp.where(low == tiles, high_before, after + tiles - 1),
        )

    def shared(*steps):
        for d in steps:
            share(d, 1 - core).wait_recv()

    parts = [arrival[i:i + TILE] for i in range(0, nz, TILE)]
    ends = {}

    def lists(index):
        if index == 0:
            loads[1].wait()
            own_block.append(layout_ref[2 * z + core])
        arrange(groups[index])

    def scale_own():
        loads[0].wait()
        scaled(plane, q_ref)

    def empty_state():
        m_s[0] = jnp.full(m_s.shape[1:], EMPTY, jnp.float32)
        al_s[0] = jnp.zeros(al_s.shape[1:], jnp.float32)

    def relay_on(r):
        for way in range(2):
            first(way, r).wait_recv()
            second(way, r).start()

    def scale_other():
        for r in range(2):
            for way in range(2):
                second(way, r).wait_recv()
        scaled(1 - plane, qx)

    def near(begin, end):
        ends[0] = second_part(0, 0, 1, 3, 0, group, begin, end)

    def middle():
        ends[1] = second_part(1, ends[0][0], 2, 7, 0, group)

    work = {
        1: [scale_own, lambda: lists(0)],
        2: [lambda: relay_on(0), lambda: lists(1), lambda: lists(2), empty_state],
        3: [lambda: relay_on(1)],
        4: [scale_other, lambda: shared(1, 2), lambda: first_part(parts[0], None, 1, 0, group)],
        5: [lambda: shared(3), lambda: near(0, 2)],
        6: [lambda: near(2, 3), lambda: shared(4), lambda: first_part(parts[1], ends[0][1], 2, 0, group)],
        7: [lambda: shared(5), middle, lambda: shared(6), lambda: first_part(parts[2], ends[1][1], 6, 0, group)],
    }

    for d in range(1, last + 1):
        for b in range(2):
            for g in range(2):
                if d < last:
                    ring(d, b, g).wait_recv()
                    if d + 1 < last:
                        ring(d + 1, b, g).start()
                    else:

                        @pl.when(core == b)
                        def _():
                            ring(last, b, g).start()
                else:

                    @pl.when(core == b)
                    def _():
                        ring(last, b, g).wait_recv()
                if (b, g) == (1, 1):
                    share(d, core).start()
        for task in work.get(d, ()):
            task()
    low_at, high_at = ends[1][0], 6
    shared(last - 1, last)

    lane = lax.broadcasted_iota(jnp.int32, (tok, HEAD_SIZE), 1)
    mine = plane * heads + h
    far_first = sorted(range(1, 2 * heads), key=lambda e: (e % heads) not in (0, 2, 6))

    def spread(buffer, landing, index):
        for e in far_first:
            p, j = outward(e)
            send(
                buffer.at[p * heads + j], landing.at[mine], o_send.at[index], o_recv.at[index], device(e)
            ).start()
        pltpu.make_async_copy(buffer.at[mine], landing.at[mine], o_recv.at[index]).start()

    lse[...] = jnp.zeros_like(lse)

    def chunk_step(chunk, _):
        offset = chunk * per_chunk
        first_part(parts[3], high_at, 9, offset, per_chunk)
        ends = second_part(2, low_at, 9, 10, offset, per_chunk)
        for side in range(2):
            for n in range(per_chunk):
                m, al = m_s[ends[side], offset + n], al_s[ends[side], offset + n]
                total = al[:, HEAD_SIZE:]
                some = total > 0.0
                safe = jnp.where(some, total, 1.0)
                mixed = (al[:, :HEAD_SIZE] / safe).astype(jnp.bfloat16)
                out_send[chunk, side * heads:(side + 1) * heads, :, n * HEAD_SIZE:(n + 1) * HEAD_SIZE] = (
                    mixed.reshape(heads, piece, HEAD_SIZE)
                )
                level = jnp.where(some, m + jnp.log2(safe), EMPTY)
                lse[side] = jnp.where(lax.rem(lane, group) == offset + n, level, lse[side])

        @pl.when(chunk < CHUNKS - 1)
        def _():
            spread(out_send.at[chunk], out_recv.at[chunk], chunk)

        return 0

    lax.fori_loop(0, CHUNKS, chunk_step, 0)

    for side in range(2):
        level = lse[side]
        high = level.astype(jnp.bfloat16).astype(jnp.float32)
        rest = (level - high).astype(jnp.bfloat16).astype(jnp.float32)
        low = level - high - rest
        packed = jnp.where(lane < group, high, jnp.where(lane < 2 * group, rest, low)).astype(jnp.bfloat16)
        stat_send[side * heads:(side + 1) * heads] = packed.reshape(heads, piece, HEAD_SIZE)
    spread(stat_send, stat_recv, CHUNKS)
    spread(out_send.at[CHUNKS - 1], out_recv.at[CHUNKS - 1], CHUNKS - 1)

    for d in range(1, last + 1):
        share(d, core).wait_send()
    for g in range(2):

        @pl.when(core != plane)
        def _():
            abroad(g).wait_send()

        @pl.when(core == plane)
        def _():
            home(g).wait_send()

        for b in range(2):
            for d in range(1, last):
                ring(d, b, g).wait_send()

            @pl.when(core == b)
            def _():
                ring(last, b, g).wait_send()
    pass_on().wait_send()
    for r in range(2):
        for way in range(2):
            first(way, r).wait_send()
            second(way, r).wait_send()

    pltpu.make_async_copy(stat_send, stat_recv, o_recv.at[CHUNKS]).wait()
    portions = []
    for source in range(heads):
        levels = []
        for side in range(2):
            packed = stat_recv[side * heads + source].astype(jnp.float32)
            levels.append(
                packed + pltpu.roll(packed, HEAD_SIZE - group, 1) + pltpu.roll(packed, HEAD_SIZE - 2 * group, 1)
            )
        portions.append(1.0 / (1.0 + jnp.exp2(levels[1] - levels[0])))
    for chunk in range(CHUNKS):
        pltpu.make_async_copy(out_send.at[chunk], out_recv.at[chunk], o_recv.at[chunk]).wait()
        for source in range(heads):
            for n in range(per_chunk):
                head = chunk * per_chunk + n
                columns = slice(n * HEAD_SIZE, (n + 1) * HEAD_SIZE)
                part_0 = out_recv[chunk, source, :, columns].astype(jnp.float32)
                part_1 = out_recv[chunk, heads + source, :, columns].astype(jnp.float32)
                portion = jnp.broadcast_to(portions[source][:, head:head + 1], (piece, HEAD_SIZE))
                start = (source * group + head) * HEAD_SIZE
                out_ref[:, start:start + HEAD_SIZE] = (part_1 + portion * (part_0 - part_1)).astype(jnp.bfloat16)

    others = pl.ds(0, 2 * heads - 1)
    pltpu.make_async_copy(stat_send.at[others], stat_recv.at[others], o_send.at[CHUNKS]).wait()
    for chunk in range(CHUNKS):
        pltpu.make_async_copy(out_send.at[chunk, others], out_recv.at[chunk, others], o_send.at[chunk]).wait()


def solution(mesh):
    nz, heads = mesh.shape["seq"] // 4, mesh.shape["head"]
    arrival = [0] + [slot for d in range(1, nz // 2) for slot in (d, nz - d)] + [nz // 2]
    groups = (arrival[:2 * TILE - 1], arrival[2 * TILE - 1:3 * TILE - 1], arrival[3 * TILE - 1:])

    def per_device(queries, keys, values, layout):
        tok, width = queries.shape
        group = width // HEAD_SIZE
        piece = tok // heads
        entries = sum(tiles_for(slots) for slots in groups) * TILE
        states = 1 + nz // TILE + entries // TILE
        bf16, f32, dma = jnp.bfloat16, jnp.float32, pltpu.SemaphoreType.DMA
        hbm = pl.BlockSpec(memory_space=pltpu.HBM)

        return pl.pallas_call(
            lambda *refs: kernel(nz, heads, arrival, groups, *refs),
            out_shape=jax.ShapeDtypeStruct((piece, heads * width), bf16),
            in_specs=[hbm] * 4,
            out_specs=pl.BlockSpec(memory_space=pltpu.VMEM),
            scratch_shapes=[pltpu.VMEM((len(slots), 2, 2, tok, HEAD_SIZE), bf16) for slots in groups]
            + [
                pltpu.VMEM((tok, width), bf16),
                pltpu.VMEM((tok, width), bf16),
                pltpu.VMEM((2, 2, tok // 2, width // 2), bf16),
                pltpu.VMEM((2, group, tok, HEAD_SIZE), bf16),
                pltpu.VMEM((states, group, tok, HEAD_SIZE), f32),
                pltpu.VMEM((states, group, tok, 2 * HEAD_SIZE), f32),
                pltpu.VMEM((CHUNKS, 2 * heads, piece, width // CHUNKS), bf16),
                pltpu.VMEM((CHUNKS, 2 * heads, piece, width // CHUNKS), bf16),
                pltpu.VMEM((2 * heads, piece, HEAD_SIZE), bf16),
                pltpu.VMEM((2 * heads, piece, HEAD_SIZE), bf16),
                pltpu.VMEM((2, tok, HEAD_SIZE), f32),
                pltpu.SMEM(layout.shape, jnp.int32),
                pltpu.SMEM((entries,), jnp.int32),
                pltpu.SMEM((entries,), jnp.int32),
                pltpu.SMEM((3, 2 * TILE), jnp.int32),
                dma((nz // 2, 2, 2)), dma((nz // 2, 2, 2)), dma((nz // 2,)), dma((nz // 2,)), dma((2, 2)), dma((2, 2)),
                dma((2, 2)), dma((2, 2)), dma((2, 2)), dma((2, 2)),
                dma((CHUNKS + 1,)), dma((CHUNKS + 1,)), dma((4,)),
            ],
            compiler_params=pltpu.CompilerParams(
                collective_id=0, has_side_effects=True, vmem_limit_bytes=44 * 1024 * 1024
            ),
            cost_estimate=pl.CostEstimate(
                flops=4 * 2 * (nz + 1) * tok * group * tok * HEAD_SIZE,
                bytes_accessed=4 * tok * width,
                transcendentals=2 * (nz + 1) * tok * group * tok,
            ),
        )(*(pltpu.with_memory_space_constraint(a, pltpu.HBM) for a in (layout, queries, keys, values)))

    return jax.shard_map(
        per_device,
        mesh=mesh,
        in_specs=(P("seq", "head"), P("seq", "head"), P("seq", "head"), P()),
        out_specs=P(("seq", "head"), None),
        check_vma=False,
    )
```

```python
import math

import jax
import jax.numpy as jnp
from jax import lax
from jax.experimental import pallas as pl
from jax.experimental.pallas import tpu as pltpu
from jax.sharding import PartitionSpec as P


HEAD_SIZE = 128
MESH = pl.DeviceIdType.MESH
EMPTY = -1e30
SCALE = math.log2(math.e) / math.sqrt(HEAD_SIZE)
CHUNKS = 2
TILE = 4


def tiles_for(slots):
    return (len(slots) + (0 in slots) - 2) // TILE + 2


def places(nz, heads):
    seq, h = lax.axis_index("seq"), lax.axis_index("head")
    return seq // (2 * nz), (seq // 2) % nz, seq % 2, h


def send(src, dst, send_sem, recv_sem, device):
    return pltpu.make_async_remote_copy(
        src_ref=src, dst_ref=dst, send_sem=send_sem, recv_sem=recv_sem, device_id=device, device_id_type=MESH
    )


def kernel(
    nz, heads, arrival, groups, layout_hbm, q_hbm, k_ref, v_ref, out_ref,
    kv_0, kv_1, kv_2, q_ref, qx, qs, m_s, al_s, out_send, out_recv, stat_send, stat_recv, lse,
    layout_ref, pick, limit, place,
    ring_send, ring_recv, share_send, share_recv, cross_send, cross_recv,
    first_send, first_recv, o_send, o_recv, local,
):
    tok, width = q_ref.shape
    group = width // HEAD_SIZE
    per_chunk = group // CHUNKS
    piece = tok // heads
    plane, z, core, h = places(nz, heads)
    last = nz // 2

    def at(p, zz, cc):
        return (p * nz + zz) * 2 + cc

    step_to = jnp.where(core == 0, 1, nz - 1)
    onward, backward = (at(plane, (z + step_to) % nz, core), h), (at(plane, (z + nz - step_to) % nz, core), h)
    sibling = (at(plane, z, 1 - core), h)
    opposite = [(at(1 - plane, z, cc), h) for cc in range(2)]
    partner = (at(1 - plane, z, core), h)

    def outward(e):
        y, half, x = (h // 4 + e // 4) % 2, (h // 2 + e // 2) % 2, (h + e) % 2
        return (plane + e // 8) % 2, y * 4 + half * 2 + x

    def device(e):
        p, j = outward(e)
        return at(p, z, core), j

    buffers = (kv_0, kv_1, kv_2)

    def spot(d, whose):
        if d == 0:
            return kv_0, 0
        if d == last:
            return kv_2, len(groups[2]) - 1
        index = 2 * d - 1 + whose
        for buffer, slots, begin in zip(buffers, groups, (0, len(groups[0]), len(groups[0]) + len(groups[1]))):
            if begin <= 2 * d - 1 < begin + len(slots):
                return buffer, index - begin

    where = {slot: (buffer, n) for buffer, slots in zip(buffers, groups) for n, slot in enumerate(slots)}

    def block(slot, whose, g):
        buffer, n = where[slot]
        return buffer.at[n, whose, g]

    sides = (plane, 1 - plane)

    def granule(d, b, g):
        buffer, n = spot(d, core)
        return buffer.at[n, sides[b], g if b == 0 else (core + g) % 2]

    def own(g):
        return pltpu.make_async_copy((k_ref, v_ref)[g], granule(0, 0, g), local.at[g])

    loads = (
        pltpu.make_async_copy(q_hbm, q_ref, local.at[2]),
        pltpu.make_async_copy(layout_hbm, layout_ref, local.at[3]),
    )

    @pl.when(core == plane)
    def _():
        for g in range(2):
            own(g).start()

    for load in loads:
        load.start()

    barrier = pltpu.get_barrier_semaphore()
    around = [onward, backward, sibling, (at(1 - plane, z, 1 - core), h)] + [device(e) for e in range(1, 2 * heads)]
    for to in around:
        pl.semaphore_signal(barrier, inc=1, device_id=to, device_id_type=MESH)
    pl.semaphore_wait(barrier, len(around))

    def ring(d, b, g):
        return send(
            granule(d - 1, b, g), granule(d, b, g), ring_send.at[d - 1, b, g], ring_recv.at[d - 1, b, g], onward
        )

    def share(d, whose):
        buffer, n = spot(d, whose)
        ref = buffer.at[n, jnp.where(whose == 0, plane, 1 - plane)] if d == last else buffer.at[n]
        return send(ref, ref, share_send.at[d - 1], share_recv.at[d - 1], sibling)

    def home(g):
        return send((k_ref, v_ref)[g], granule(0, 0, g), cross_send.at[0, g], cross_recv.at[0, g], sibling)

    def abroad(g):
        return send((k_ref, v_ref)[g], kv_0.at[0, plane, g], cross_send.at[0, g], cross_recv.at[1, 0], opposite[g])

    def pass_on():
        return send(granule(0, 1, 0), granule(0, 1, 0), cross_send.at[1, 0], cross_recv.at[1, 1], sibling)

    def passed():
        return send(granule(0, 1, 1), granule(0, 1, 1), cross_send.at[1, 0], cross_recv.at[1, 1], sibling)

    def hand_over():
        return send(q_hbm, qx, first_send.at[0], first_recv.at[0], partner)

    @pl.when(core != plane)
    def _():
        for g in range(2):
            abroad(g).start()

    @pl.when(core == plane)
    def _():
        for g in range(2):
            home(g).start()

    for g in range(2):

        @pl.when(core != plane)
        def _():
            home(g).wait_recv()

        @pl.when(core == plane)
        def _():
            own(g).wait()

        ring(1, 0, g).start()
    send(k_ref, granule(0, 1, 0), cross_send.at[0, 0], cross_recv.at[1, 0], opposite[0]).wait_recv()
    ring(1, 1, 0).start()
    pass_on().start()
    hand_over().start()
    passed().wait_recv()
    ring(1, 1, 1).start()

    own_block, low_tiles, starts, tile_counts = [], [], [], []

    def arrange(slots):
        tiles, start = tiles_for(slots), sum(tile_counts) * TILE
        positions = [layout_ref[2 * ((z + nz - slot) % nz) + plane] for slot in slots]
        count = jnp.int32(0)
        for position in positions:
            count += (position <= own_block[0]).astype(jnp.int32)
        low = (count + TILE - 1) // TILE
        low_next, high_next = jnp.int32(0), low * TILE
        for n, position in enumerate(positions):
            is_low, is_high = position <= own_block[0], position >= own_block[0]
            place[0, n] = jnp.where(is_low, low_next, -1)
            place[1, n] = jnp.where(is_high, high_next, -1)
            place[2, n] = jnp.where(position == own_block[0], 0, tok)
            low_next += is_low.astype(jnp.int32)
            high_next += is_high.astype(jnp.int32)

        def order(t, _):
            index, bound = jnp.int32(0), jnp.int32(-tok)
            for n in range(len(slots)):
                here = (place[0, n] == t) | (place[1, n] == t)
                index = jnp.where(here, n, index)
                bound = jnp.where(here, place[2, n], bound)
            pick[start + t] = index
            limit[start + t] = bound
            return 0

        lax.fori_loop(0, tiles * TILE, order, 0)
        low_tiles.append(low)
        starts.append(start)
        tile_counts.append(tiles)

    def scaled(target, ref):
        for head in range(group):
            part = ref[:, head * HEAD_SIZE:(head + 1) * HEAD_SIZE].astype(jnp.float32) * SCALE
            qs[target, head] = part.astype(jnp.bfloat16)

    ones = jnp.ones((TILE * tok, HEAD_SIZE), jnp.bfloat16)

    def tile(side, keys, values, before, after, bounds, offset, count):
        values = jnp.concatenate([values, ones], axis=1)

        def scores(n):
            return lax.dot_general(
                qs[side, offset + n], keys, (((1,), (1,)), ((), ())), preferred_element_type=jnp.float32
            )

        if bounds is not None:
            ahead = lax.broadcasted_iota(jnp.int32, (tok, tok), 1) - lax.broadcasted_iota(jnp.int32, (tok, tok), 0)
        upcoming = scores(0)
        for n in range(count):
            score = upcoming
            if n + 1 < count:
                upcoming = scores(n + 1)
            parts = [score[:, j * tok:(j + 1) * tok] for j in range(TILE)]
            if bounds is not None:
                parts = [jnp.where(ahead <= bounds[j], parts[j], EMPTY) for j in range(TILE)]
            widest = parts[0]
            for part in parts[1:]:
                widest = jnp.maximum(widest, part)
            top = jnp.max(widest, axis=1, keepdims=True)
            if before is None:
                m_next = jnp.broadcast_to(top, (tok, HEAD_SIZE))
            else:
                m = m_s[before, offset + n]
                m_next = jnp.maximum(m, top)
            weight = jnp.concatenate([jnp.exp2(part - m_next).astype(jnp.bfloat16) for part in parts], axis=1)
            mixed = jnp.dot(weight, values, preferred_element_type=jnp.float32)
            if before is not None:
                factor = jnp.exp2(m - m_next)
                mixed += al_s[before, offset + n] * jnp.concatenate([factor, factor], axis=1)
            m_s[after, offset + n] = m_next
            al_s[after, offset + n] = mixed

    def first_part(slots, before, after, offset, count):
        keys = jnp.concatenate([block(slot, 0, 0)[...] for slot in slots], axis=0)
        values = jnp.concatenate([block(slot, 0, 1)[...] for slot in slots], axis=0)
        tile(1, keys, values, before, after, None, offset, count)

    def second_part(index, low_before, high_before, after, offset, count, begin=0, end=None):
        buffer, low, base, tiles = buffers[index], low_tiles[index], starts[index], tile_counts[index]

        def step(t, _):
            side = jnp.where(t < low, 0, 1)
            before = jnp.where(t == low, high_before, jnp.where(t == 0, low_before, after + t - 1))
            chosen = [pick[base + t * TILE + j] for j in range(TILE)]
            bounds = [limit[base + t * TILE + j] for j in range(TILE)]
            keys = jnp.concatenate([buffer[n, side, 0] for n in chosen], axis=0)
            values = jnp.concatenate([buffer[n, side, 1] for n in chosen], axis=0)
            tile(side, keys, values, before, after + t, bounds, offset, count)
            return 0

        lax.fori_loop(begin, tiles if end is None else end, step, 0)
        return (
            jnp.where(low == 0, low_before, after + low - 1),
            jnp.where(low == tiles, high_before, after + tiles - 1),
        )

    def shared(*steps):
        for d in steps:
            share(d, 1 - core).wait_recv()

    parts = [arrival[i:i + TILE] for i in range(0, nz, TILE)]
    ends = {}

    def lists(index):
        if index == 0:
            loads[1].wait()
            own_block.append(layout_ref[2 * z + core])
        arrange(groups[index])

    def scale_own():
        loads[0].wait()
        scaled(plane, q_ref)

    def empty_state():
        m_s[0] = jnp.full(m_s.shape[1:], EMPTY, jnp.float32)
        al_s[0] = jnp.zeros(al_s.shape[1:], jnp.float32)

    def scale_other():
        hand_over().wait_recv()
        scaled(1 - plane, qx)

    def near(begin, end):
        ends[0] = second_part(0, 0, 1, 3, 0, group, begin, end)

    def middle():
        ends[1] = second_part(1, ends[0][0], 2, 7, 0, group)

    work = {
        1: [scale_own, lambda: lists(0)],
        2: [lambda: lists(1), lambda: lists(2)],
        3: [empty_state],
        4: [scale_other, lambda: shared(1, 2), lambda: first_part(parts[0], None, 1, 0, group)],
        5: [lambda: shared(3), lambda: near(0, 2)],
        6: [lambda: near(2, 3), lambda: shared(4), lambda: first_part(parts[1], ends[0][1], 2, 0, group)],
        7: [lambda: shared(5), middle, lambda: shared(6), lambda: first_part(parts[2], ends[1][1], 6, 0, group)],
    }

    for d in range(1, last + 1):
        for b in range(2):
            for g in range(2):
                if d < last:
                    ring(d, b, g).wait_recv()
                    if d + 1 < last:
                        ring(d + 1, b, g).start()
                    else:

                        @pl.when(core == b)
                        def _():
                            ring(last, b, g).start()
                else:

                    @pl.when(core == b)
                    def _():
                        ring(last, b, g).wait_recv()
                if (b, g) == (1, 1):
                    share(d, core).start()
        for task in work.get(d, ()):
            task()
    low_at, high_at = ends[1][0], 6
    shared(last - 1, last)

    lane = lax.broadcasted_iota(jnp.int32, (tok, HEAD_SIZE), 1)
    mine = plane * heads + h
    far_first = sorted(range(1, 2 * heads), key=lambda e: -(e // 8 + e // 2 % 2))

    def spread(buffer, landing, index):
        for e in far_first:
            p, j = outward(e)
            send(
                buffer.at[p * heads + j], landing.at[mine], o_send.at[index], o_recv.at[index], device(e)
            ).start()
        pltpu.make_async_copy(buffer.at[mine], landing.at[mine], o_recv.at[index]).start()

    lse[...] = jnp.zeros_like(lse)

    def chunk_step(chunk, _):
        offset = chunk * per_chunk
        first_part(parts[3], high_at, 9, offset, per_chunk)
        ends = second_part(2, low_at, 9, 10, offset, per_chunk)
        for side in range(2):
            for n in range(per_chunk):
                m, al = m_s[ends[side], offset + n], al_s[ends[side], offset + n]
                total = al[:, HEAD_SIZE:]
                some = total > 0.0
                safe = jnp.where(some, total, 1.0)
                mixed = (al[:, :HEAD_SIZE] / safe).astype(jnp.bfloat16)
                out_send[chunk, side * heads:(side + 1) * heads, :, n * HEAD_SIZE:(n + 1) * HEAD_SIZE] = (
                    mixed.reshape(heads, piece, HEAD_SIZE)
                )
                level = jnp.where(some, m + jnp.log2(safe), EMPTY)
                lse[side] = jnp.where(lax.rem(lane, group) == offset + n, level, lse[side])

        @pl.when(chunk < CHUNKS - 1)
        def _():
            spread(out_send.at[chunk], out_recv.at[chunk], chunk)

        return 0

    lax.fori_loop(0, CHUNKS, chunk_step, 0)

    for side in range(2):
        level = lse[side]
        high = level.astype(jnp.bfloat16).astype(jnp.float32)
        rest = (level - high).astype(jnp.bfloat16).astype(jnp.float32)
        low = level - high - rest
        packed = jnp.where(lane < group, high, jnp.where(lane < 2 * group, rest, low)).astype(jnp.bfloat16)
        stat_send[side * heads:(side + 1) * heads] = packed.reshape(heads, piece, HEAD_SIZE)
    spread(stat_send, stat_recv, CHUNKS)
    spread(out_send.at[CHUNKS - 1], out_recv.at[CHUNKS - 1], CHUNKS - 1)

    for d in range(1, last + 1):
        share(d, core).wait_send()
    for g in range(2):

        @pl.when(core != plane)
        def _():
            abroad(g).wait_send()

        @pl.when(core == plane)
        def _():
            home(g).wait_send()

        for b in range(2):
            for d in range(1, last):
                ring(d, b, g).wait_send()

            @pl.when(core == b)
            def _():
                ring(last, b, g).wait_send()
    pass_on().wait_send()
    hand_over().wait_send()

    pltpu.make_async_copy(stat_send, stat_recv, o_recv.at[CHUNKS]).wait()
    portions = []
    for source in range(heads):
        levels = []
        for side in range(2):
            packed = stat_recv[side * heads + source].astype(jnp.float32)
            levels.append(
                packed + pltpu.roll(packed, HEAD_SIZE - group, 1) + pltpu.roll(packed, HEAD_SIZE - 2 * group, 1)
            )
        portions.append(1.0 / (1.0 + jnp.exp2(levels[1] - levels[0])))
    for chunk in range(CHUNKS):
        pltpu.make_async_copy(out_send.at[chunk], out_recv.at[chunk], o_recv.at[chunk]).wait()
        for source in range(heads):
            for n in range(per_chunk):
                head = chunk * per_chunk + n
                columns = slice(n * HEAD_SIZE, (n + 1) * HEAD_SIZE)
                part_0 = out_recv[chunk, source, :, columns].astype(jnp.float32)
                part_1 = out_recv[chunk, heads + source, :, columns].astype(jnp.float32)
                portion = jnp.broadcast_to(portions[source][:, head:head + 1], (piece, HEAD_SIZE))
                start = (source * group + head) * HEAD_SIZE
                out_ref[:, start:start + HEAD_SIZE] = (part_1 + portion * (part_0 - part_1)).astype(jnp.bfloat16)

    others = pl.ds(0, 2 * heads - 1)
    pltpu.make_async_copy(stat_send.at[others], stat_recv.at[others], o_send.at[CHUNKS]).wait()
    for chunk in range(CHUNKS):
        pltpu.make_async_copy(out_send.at[chunk, others], out_recv.at[chunk, others], o_send.at[chunk]).wait()


def solution(mesh):
    nz, heads = mesh.shape["seq"] // 4, mesh.shape["head"]
    arrival = [0] + [slot for d in range(1, nz // 2) for slot in (d, nz - d)] + [nz // 2]
    groups = (arrival[:2 * TILE - 1], arrival[2 * TILE - 1:3 * TILE - 1], arrival[3 * TILE - 1:])

    def per_device(queries, keys, values, layout):
        tok, width = queries.shape
        group = width // HEAD_SIZE
        piece = tok // heads
        entries = sum(tiles_for(slots) for slots in groups) * TILE
        states = 1 + nz // TILE + entries // TILE
        bf16, f32, dma = jnp.bfloat16, jnp.float32, pltpu.SemaphoreType.DMA
        hbm = pl.BlockSpec(memory_space=pltpu.HBM)

        return pl.pallas_call(
            lambda *refs: kernel(nz, heads, arrival, groups, *refs),
            out_shape=jax.ShapeDtypeStruct((piece, heads * width), bf16),
            in_specs=[hbm] * 4,
            out_specs=pl.BlockSpec(memory_space=pltpu.VMEM),
            scratch_shapes=[pltpu.VMEM((len(slots), 2, 2, tok, HEAD_SIZE), bf16) for slots in groups]
            + [
                pltpu.VMEM((tok, width), bf16),
                pltpu.VMEM((tok, width), bf16),
                pltpu.VMEM((2, group, tok, HEAD_SIZE), bf16),
                pltpu.VMEM((states, group, tok, HEAD_SIZE), f32),
                pltpu.VMEM((states, group, tok, 2 * HEAD_SIZE), f32),
                pltpu.VMEM((CHUNKS, 2 * heads, piece, width // CHUNKS), bf16),
                pltpu.VMEM((CHUNKS, 2 * heads, piece, width // CHUNKS), bf16),
                pltpu.VMEM((2 * heads, piece, HEAD_SIZE), bf16),
                pltpu.VMEM((2 * heads, piece, HEAD_SIZE), bf16),
                pltpu.VMEM((2, tok, HEAD_SIZE), f32),
                pltpu.SMEM(layout.shape, jnp.int32),
                pltpu.SMEM((entries,), jnp.int32),
                pltpu.SMEM((entries,), jnp.int32),
                pltpu.SMEM((3, 2 * TILE), jnp.int32),
                dma((nz // 2, 2, 2)), dma((nz // 2, 2, 2)), dma((nz // 2,)), dma((nz // 2,)), dma((2, 2)), dma((2, 2)),
                dma((1,)), dma((1,)),
                dma((CHUNKS + 1,)), dma((CHUNKS + 1,)), dma((4,)),
            ],
            compiler_params=pltpu.CompilerParams(
                collective_id=0, has_side_effects=True, vmem_limit_bytes=44 * 1024 * 1024
            ),
            cost_estimate=pl.CostEstimate(
                flops=4 * 2 * (nz + 1) * tok * group * tok * HEAD_SIZE,
                bytes_accessed=4 * tok * width,
                transcendentals=2 * (nz + 1) * tok * group * tok,
            ),
        )(*(pltpu.with_memory_space_constraint(a, pltpu.HBM) for a in (layout, queries, keys, values)))

    return jax.shard_map(
        per_device,
        mesh=mesh,
        in_specs=(P("seq", "head"), P("seq", "head"), P("seq", "head"), P()),
        out_specs=P(("seq", "head"), None),
        check_vma=False,
    )
```

```python
import math

import jax
import jax.numpy as jnp
from jax import lax
from jax.experimental import pallas as pl
from jax.experimental.pallas import tpu as pltpu
from jax.sharding import PartitionSpec as P


HEAD_SIZE = 128
MESH = pl.DeviceIdType.MESH
EMPTY = -1e30
SCALE = math.log2(math.e) / math.sqrt(HEAD_SIZE)
CHUNKS = 4
TILE = 4


def tiles_for(slots):
    return (len(slots) + (0 in slots) - 2) // TILE + 2


def places(nz, heads):
    seq, h = lax.axis_index("seq"), lax.axis_index("head")
    return seq // (2 * nz), (seq // 2) % nz, seq % 2, h


def send(src, dst, send_sem, recv_sem, device):
    return pltpu.make_async_remote_copy(
        src_ref=src, dst_ref=dst, send_sem=send_sem, recv_sem=recv_sem, device_id=device, device_id_type=MESH
    )


def kernel(
    nz, heads, arrival, groups, layout_hbm, q_hbm, k_ref, v_ref, out_ref,
    kv_0, kv_1, kv_2, q_ref, qx, qs, m_s, al_s, out_send, out_recv, stat_send, stat_recv, lse,
    layout_ref, pick, limit, place,
    ring_send, ring_recv, share_send, share_recv, cross_send, cross_recv,
    first_send, first_recv, o_send, o_recv, local,
):
    tok, width = q_ref.shape
    group = width // HEAD_SIZE
    per_chunk = group // CHUNKS
    piece = tok // heads
    plane, z, core, h = places(nz, heads)
    last = nz // 2

    def at(p, zz, cc):
        return (p * nz + zz) * 2 + cc

    step_to = jnp.where(core == 0, 1, nz - 1)
    onward, backward = (at(plane, (z + step_to) % nz, core), h), (at(plane, (z + nz - step_to) % nz, core), h)
    sibling = (at(plane, z, 1 - core), h)
    opposite = [(at(1 - plane, z, cc), h) for cc in range(2)]
    partner = (at(1 - plane, z, core), h)

    def outward(e):
        y, half, x = (h // 4 + e // 4) % 2, (h // 2 + e // 2) % 2, (h + e) % 2
        return (plane + e // 8) % 2, y * 4 + half * 2 + x

    def device(e):
        p, j = outward(e)
        return at(p, z, core), j

    buffers = (kv_0, kv_1, kv_2)

    def spot(d, whose):
        if d == 0:
            return kv_0, 0
        if d == last:
            return kv_2, len(groups[2]) - 1
        index = 2 * d - 1 + whose
        for buffer, slots, begin in zip(buffers, groups, (0, len(groups[0]), len(groups[0]) + len(groups[1]))):
            if begin <= 2 * d - 1 < begin + len(slots):
                return buffer, index - begin

    where = {slot: (buffer, n) for buffer, slots in zip(buffers, groups) for n, slot in enumerate(slots)}

    def block(slot, whose, g):
        buffer, n = where[slot]
        return buffer.at[n, whose, g]

    sides = (plane, 1 - plane)

    def granule(d, b, g):
        buffer, n = spot(d, core)
        return buffer.at[n, sides[b], g if b == 0 else (core + g) % 2]

    def own(g):
        return pltpu.make_async_copy((k_ref, v_ref)[g], granule(0, 0, g), local.at[g])

    loads = (
        pltpu.make_async_copy(q_hbm, q_ref, local.at[2]),
        pltpu.make_async_copy(layout_hbm, layout_ref, local.at[3]),
    )

    @pl.when(core == plane)
    def _():
        for g in range(2):
            own(g).start()

    for load in loads:
        load.start()

    barrier = pltpu.get_barrier_semaphore()
    around = [onward, backward, sibling, (at(1 - plane, z, 1 - core), h)] + [device(e) for e in range(1, 2 * heads)]
    for to in around:
        pl.semaphore_signal(barrier, inc=1, device_id=to, device_id_type=MESH)
    pl.semaphore_wait(barrier, len(around))

    def ring(d, b, g):
        return send(
            granule(d - 1, b, g), granule(d, b, g), ring_send.at[d - 1, b, g], ring_recv.at[d - 1, b, g], onward
        )

    def share(d, whose):
        buffer, n = spot(d, whose)
        ref = buffer.at[n, jnp.where(whose == 0, plane, 1 - plane)] if d == last else buffer.at[n]
        return send(ref, ref, share_send.at[d - 1], share_recv.at[d - 1], sibling)

    def home(g):
        return send((k_ref, v_ref)[g], granule(0, 0, g), cross_send.at[0, g], cross_recv.at[0, g], sibling)

    def abroad(g):
        return send((k_ref, v_ref)[g], kv_0.at[0, plane, g], cross_send.at[0, g], cross_recv.at[1, 0], opposite[g])

    def pass_on():
        return send(granule(0, 1, 0), granule(0, 1, 0), cross_send.at[1, 0], cross_recv.at[1, 1], sibling)

    def passed():
        return send(granule(0, 1, 1), granule(0, 1, 1), cross_send.at[1, 0], cross_recv.at[1, 1], sibling)

    def hand_over():
        return send(q_hbm, qx, first_send.at[0], first_recv.at[0], partner)

    @pl.when(core != plane)
    def _():
        for g in range(2):
            abroad(g).start()

    @pl.when(core == plane)
    def _():
        for g in range(2):
            home(g).start()

    for g in range(2):

        @pl.when(core != plane)
        def _():
            home(g).wait_recv()

        @pl.when(core == plane)
        def _():
            own(g).wait()

        ring(1, 0, g).start()
    send(k_ref, granule(0, 1, 0), cross_send.at[0, 0], cross_recv.at[1, 0], opposite[0]).wait_recv()
    ring(1, 1, 0).start()
    pass_on().start()
    hand_over().start()
    passed().wait_recv()
    ring(1, 1, 1).start()

    own_block, low_tiles, starts, tile_counts = [], [], [], []

    def arrange(slots):
        tiles, start = tiles_for(slots), sum(tile_counts) * TILE
        positions = [layout_ref[2 * ((z + nz - slot) % nz) + plane] for slot in slots]
        count = jnp.int32(0)
        for position in positions:
            count += (position <= own_block[0]).astype(jnp.int32)
        low = (count + TILE - 1) // TILE
        low_next, high_next = jnp.int32(0), low * TILE
        for n, position in enumerate(positions):
            is_low, is_high = position <= own_block[0], position >= own_block[0]
            place[0, n] = jnp.where(is_low, low_next, -1)
            place[1, n] = jnp.where(is_high, high_next, -1)
            place[2, n] = jnp.where(position == own_block[0], 0, tok)
            low_next += is_low.astype(jnp.int32)
            high_next += is_high.astype(jnp.int32)

        def order(t, _):
            index, bound = jnp.int32(0), jnp.int32(-tok)
            for n in range(len(slots)):
                here = (place[0, n] == t) | (place[1, n] == t)
                index = jnp.where(here, n, index)
                bound = jnp.where(here, place[2, n], bound)
            pick[start + t] = index
            limit[start + t] = bound
            return 0

        lax.fori_loop(0, tiles * TILE, order, 0)
        low_tiles.append(low)
        starts.append(start)
        tile_counts.append(tiles)

    def scaled(target, ref):
        for head in range(group):
            part = ref[:, head * HEAD_SIZE:(head + 1) * HEAD_SIZE].astype(jnp.float32) * SCALE
            qs[target, head] = part.astype(jnp.bfloat16)

    ones = jnp.ones((TILE * tok, HEAD_SIZE), jnp.bfloat16)

    def tile(side, keys, values, before, after, bounds, offset, count):
        values = jnp.concatenate([values, ones], axis=1)

        def scores(n):
            return lax.dot_general(
                qs[side, offset + n], keys, (((1,), (1,)), ((), ())), preferred_element_type=jnp.float32
            )

        if bounds is not None:
            ahead = lax.broadcasted_iota(jnp.int32, (tok, tok), 1) - lax.broadcasted_iota(jnp.int32, (tok, tok), 0)
        upcoming = scores(0)
        for n in range(count):
            score = upcoming
            if n + 1 < count:
                upcoming = scores(n + 1)
            parts = [score[:, j * tok:(j + 1) * tok] for j in range(TILE)]
            if bounds is not None:
                parts = [jnp.where(ahead <= bounds[j], parts[j], EMPTY) for j in range(TILE)]
            widest = parts[0]
            for part in parts[1:]:
                widest = jnp.maximum(widest, part)
            top = jnp.max(widest, axis=1, keepdims=True)
            if before is None:
                m_next = jnp.broadcast_to(top, (tok, HEAD_SIZE))
            else:
                m = m_s[before, offset + n]
                m_next = jnp.maximum(m, top)
            weight = jnp.concatenate([jnp.exp2(part - m_next).astype(jnp.bfloat16) for part in parts], axis=1)
            mixed = jnp.dot(weight, values, preferred_element_type=jnp.float32)
            if before is not None:
                factor = jnp.exp2(m - m_next)
                mixed += al_s[before, offset + n] * jnp.concatenate([factor, factor], axis=1)
            m_s[after, offset + n] = m_next
            al_s[after, offset + n] = mixed

    def first_part(slots, before, after, offset, count):
        keys = jnp.concatenate([block(slot, 0, 0)[...] for slot in slots], axis=0)
        values = jnp.concatenate([block(slot, 0, 1)[...] for slot in slots], axis=0)
        tile(1, keys, values, before, after, None, offset, count)

    def second_part(index, low_before, high_before, after, offset, count, begin=0, end=None):
        buffer, low, base, tiles = buffers[index], low_tiles[index], starts[index], tile_counts[index]

        def step(t, _):
            side = jnp.where(t < low, 0, 1)
            before = jnp.where(t == low, high_before, jnp.where(t == 0, low_before, after + t - 1))
            chosen = [pick[base + t * TILE + j] for j in range(TILE)]
            bounds = [limit[base + t * TILE + j] for j in range(TILE)]
            keys = jnp.concatenate([buffer[n, side, 0] for n in chosen], axis=0)
            values = jnp.concatenate([buffer[n, side, 1] for n in chosen], axis=0)
            tile(side, keys, values, before, after + t, bounds, offset, count)
            return 0

        lax.fori_loop(begin, tiles if end is None else end, step, 0)
        return (
            jnp.where(low == 0, low_before, after + low - 1),
            jnp.where(low == tiles, high_before, after + tiles - 1),
        )

    def shared(*steps):
        for d in steps:
            share(d, 1 - core).wait_recv()

    parts = [arrival[i:i + TILE] for i in range(0, nz, TILE)]
    ends = {}

    def lists(index):
        if index == 0:
            loads[1].wait()
            own_block.append(layout_ref[2 * z + core])
        arrange(groups[index])

    def scale_own():
        loads[0].wait()
        scaled(plane, q_ref)

    def empty_state():
        m_s[0] = jnp.full(m_s.shape[1:], EMPTY, jnp.float32)
        al_s[0] = jnp.zeros(al_s.shape[1:], jnp.float32)

    def scale_other():
        hand_over().wait_recv()
        scaled(1 - plane, qx)

    def near(begin, end):
        ends[0] = second_part(0, 0, 1, 3, 0, group, begin, end)

    def middle():
        ends[1] = second_part(1, ends[0][0], 2, 7, 0, group)

    work = {
        1: [scale_own, lambda: lists(0)],
        2: [lambda: lists(1), lambda: lists(2)],
        3: [empty_state],
        4: [scale_other, lambda: shared(1, 2), lambda: first_part(parts[0], None, 1, 0, group)],
        5: [lambda: shared(3), lambda: near(0, 2)],
        6: [lambda: near(2, 3), lambda: shared(4), lambda: first_part(parts[1], ends[0][1], 2, 0, group)],
        7: [lambda: shared(5), middle, lambda: shared(6), lambda: first_part(parts[2], ends[1][1], 6, 0, group)],
    }

    for d in range(1, last + 1):
        for b in range(2):
            for g in range(2):
                if d < last:
                    ring(d, b, g).wait_recv()
                    if d + 1 < last:
                        ring(d + 1, b, g).start()
                    else:

                        @pl.when(core == b)
                        def _():
                            ring(last, b, g).start()
                else:

                    @pl.when(core == b)
                    def _():
                        ring(last, b, g).wait_recv()
                if (b, g) == (1, 1):
                    share(d, core).start()
        for task in work.get(d, ()):
            task()
    low_at, high_at = ends[1][0], 6
    shared(last - 1, last)

    lane = lax.broadcasted_iota(jnp.int32, (tok, HEAD_SIZE), 1)
    mine = plane * heads + h
    far_first = sorted(range(1, 2 * heads), key=lambda e: -(e // 8 + e // 2 % 2))

    def spread(buffer, landing, index):
        for e in far_first:
            p, j = outward(e)
            send(
                buffer.at[p * heads + j], landing.at[mine], o_send.at[index], o_recv.at[index], device(e)
            ).start()
        pltpu.make_async_copy(buffer.at[mine], landing.at[mine], o_recv.at[index]).start()

    lse[...] = jnp.zeros_like(lse)

    def chunk_step(chunk, _):
        offset = chunk * per_chunk
        first_part(parts[3], high_at, 9, offset, per_chunk)
        ends = second_part(2, low_at, 9, 10, offset, per_chunk)
        for side in range(2):
            for n in range(per_chunk):
                m, al = m_s[ends[side], offset + n], al_s[ends[side], offset + n]
                total = al[:, HEAD_SIZE:]
                some = total > 0.0
                safe = jnp.where(some, total, 1.0)
                mixed = (al[:, :HEAD_SIZE] / safe).astype(jnp.bfloat16)
                out_send[chunk, side * heads:(side + 1) * heads, :, n * HEAD_SIZE:(n + 1) * HEAD_SIZE] = (
                    mixed.reshape(heads, piece, HEAD_SIZE)
                )
                level = jnp.where(some, m + jnp.log2(safe), EMPTY)
                lse[side] = jnp.where(lax.rem(lane, group) == offset + n, level, lse[side])

        @pl.when(chunk < CHUNKS - 1)
        def _():
            spread(out_send.at[chunk], out_recv.at[chunk], chunk)

        return 0

    lax.fori_loop(0, CHUNKS, chunk_step, 0)

    for side in range(2):
        level = lse[side]
        high = level.astype(jnp.bfloat16).astype(jnp.float32)
        rest = (level - high).astype(jnp.bfloat16).astype(jnp.float32)
        low = level - high - rest
        packed = jnp.where(lane < group, high, jnp.where(lane < 2 * group, rest, low)).astype(jnp.bfloat16)
        stat_send[side * heads:(side + 1) * heads] = packed.reshape(heads, piece, HEAD_SIZE)
    spread(stat_send, stat_recv, CHUNKS)
    spread(out_send.at[CHUNKS - 1], out_recv.at[CHUNKS - 1], CHUNKS - 1)

    for d in range(1, last + 1):
        share(d, core).wait_send()
    for g in range(2):

        @pl.when(core != plane)
        def _():
            abroad(g).wait_send()

        @pl.when(core == plane)
        def _():
            home(g).wait_send()

        for b in range(2):
            for d in range(1, last):
                ring(d, b, g).wait_send()

            @pl.when(core == b)
            def _():
                ring(last, b, g).wait_send()
    pass_on().wait_send()
    hand_over().wait_send()

    pltpu.make_async_copy(stat_send, stat_recv, o_recv.at[CHUNKS]).wait()
    portions = []
    for source in range(heads):
        levels = []
        for side in range(2):
            packed = stat_recv[side * heads + source].astype(jnp.float32)
            levels.append(
                packed + pltpu.roll(packed, HEAD_SIZE - group, 1) + pltpu.roll(packed, HEAD_SIZE - 2 * group, 1)
            )
        portions.append(1.0 / (1.0 + jnp.exp2(levels[1] - levels[0])))
    for chunk in range(CHUNKS):
        pltpu.make_async_copy(out_send.at[chunk], out_recv.at[chunk], o_recv.at[chunk]).wait()
        for source in range(heads):
            for n in range(per_chunk):
                head = chunk * per_chunk + n
                columns = slice(n * HEAD_SIZE, (n + 1) * HEAD_SIZE)
                part_0 = out_recv[chunk, source, :, columns].astype(jnp.float32)
                part_1 = out_recv[chunk, heads + source, :, columns].astype(jnp.float32)
                portion = jnp.broadcast_to(portions[source][:, head:head + 1], (piece, HEAD_SIZE))
                start = (source * group + head) * HEAD_SIZE
                out_ref[:, start:start + HEAD_SIZE] = (part_1 + portion * (part_0 - part_1)).astype(jnp.bfloat16)

    others = pl.ds(0, 2 * heads - 1)
    pltpu.make_async_copy(stat_send.at[others], stat_recv.at[others], o_send.at[CHUNKS]).wait()
    for chunk in range(CHUNKS):
        pltpu.make_async_copy(out_send.at[chunk, others], out_recv.at[chunk, others], o_send.at[chunk]).wait()


def solution(mesh):
    nz, heads = mesh.shape["seq"] // 4, mesh.shape["head"]
    arrival = [0] + [slot for d in range(1, nz // 2) for slot in (d, nz - d)] + [nz // 2]
    groups = (arrival[:2 * TILE - 1], arrival[2 * TILE - 1:3 * TILE - 1], arrival[3 * TILE - 1:])

    def per_device(queries, keys, values, layout):
        tok, width = queries.shape
        group = width // HEAD_SIZE
        piece = tok // heads
        entries = sum(tiles_for(slots) for slots in groups) * TILE
        states = 1 + nz // TILE + entries // TILE
        bf16, f32, dma = jnp.bfloat16, jnp.float32, pltpu.SemaphoreType.DMA
        hbm = pl.BlockSpec(memory_space=pltpu.HBM)

        return pl.pallas_call(
            lambda *refs: kernel(nz, heads, arrival, groups, *refs),
            out_shape=jax.ShapeDtypeStruct((piece, heads * width), bf16),
            in_specs=[hbm] * 4,
            out_specs=pl.BlockSpec(memory_space=pltpu.VMEM),
            scratch_shapes=[pltpu.VMEM((len(slots), 2, 2, tok, HEAD_SIZE), bf16) for slots in groups]
            + [
                pltpu.VMEM((tok, width), bf16),
                pltpu.VMEM((tok, width), bf16),
                pltpu.VMEM((2, group, tok, HEAD_SIZE), bf16),
                pltpu.VMEM((states, group, tok, HEAD_SIZE), f32),
                pltpu.VMEM((states, group, tok, 2 * HEAD_SIZE), f32),
                pltpu.VMEM((CHUNKS, 2 * heads, piece, width // CHUNKS), bf16),
                pltpu.VMEM((CHUNKS, 2 * heads, piece, width // CHUNKS), bf16),
                pltpu.VMEM((2 * heads, piece, HEAD_SIZE), bf16),
                pltpu.VMEM((2 * heads, piece, HEAD_SIZE), bf16),
                pltpu.VMEM((2, tok, HEAD_SIZE), f32),
                pltpu.SMEM(layout.shape, jnp.int32),
                pltpu.SMEM((entries,), jnp.int32),
                pltpu.SMEM((entries,), jnp.int32),
                pltpu.SMEM((3, 2 * TILE), jnp.int32),
                dma((nz // 2, 2, 2)), dma((nz // 2, 2, 2)), dma((nz // 2,)), dma((nz // 2,)), dma((2, 2)), dma((2, 2)),
                dma((1,)), dma((1,)),
                dma((CHUNKS + 1,)), dma((CHUNKS + 1,)), dma((4,)),
            ],
            compiler_params=pltpu.CompilerParams(
                collective_id=0, has_side_effects=True, vmem_limit_bytes=44 * 1024 * 1024
            ),
            cost_estimate=pl.CostEstimate(
                flops=4 * 2 * (nz + 1) * tok * group * tok * HEAD_SIZE,
                bytes_accessed=4 * tok * width,
                transcendentals=2 * (nz + 1) * tok * group * tok,
            ),
        )(*(pltpu.with_memory_space_constraint(a, pltpu.HBM) for a in (layout, queries, keys, values)))

    return jax.shard_map(
        per_device,
        mesh=mesh,
        in_specs=(P("seq", "head"), P("seq", "head"), P("seq", "head"), P()),
        out_specs=P(("seq", "head"), None),
        check_vma=False,
    )
```

```python
import math

import jax
import jax.numpy as jnp
from jax import lax
from jax.experimental import pallas as pl
from jax.experimental.pallas import tpu as pltpu
from jax.sharding import PartitionSpec as P


HEAD_SIZE = 128
MESH = pl.DeviceIdType.MESH
EMPTY = -1e30
SCALE = math.log2(math.e) / math.sqrt(HEAD_SIZE)
CHUNKS = 4
TILE = 4


def tiles_for(slots):
    return (len(slots) + (0 in slots) - 2) // TILE + 2


def places(nz, heads):
    seq, h = lax.axis_index("seq"), lax.axis_index("head")
    return seq // (2 * nz), (seq // 2) % nz, seq % 2, h


def send(src, dst, send_sem, recv_sem, device):
    return pltpu.make_async_remote_copy(
        src_ref=src, dst_ref=dst, send_sem=send_sem, recv_sem=recv_sem, device_id=device, device_id_type=MESH
    )


def kernel(
    nz, heads, arrival, groups, layout_hbm, q_hbm, k_ref, v_ref, out_ref,
    kv_0, kv_1, kv_2, q_ref, qx, qs, m_s, al_s, out_send, out_recv, stat_send, stat_recv, lse,
    layout_ref, pick, limit, place,
    ring_send, ring_recv, share_send, share_recv, cross_send, cross_recv,
    first_send, first_recv, o_send, o_recv, local,
):
    tok, width = q_ref.shape
    group = width // HEAD_SIZE
    per_chunk = group // CHUNKS
    piece = tok // heads
    plane, z, core, h = places(nz, heads)
    last = nz // 2

    def at(p, zz, cc):
        return (p * nz + zz) * 2 + cc

    step_to = jnp.where(core == 0, 1, nz - 1)
    onward, backward = (at(plane, (z + step_to) % nz, core), h), (at(plane, (z + nz - step_to) % nz, core), h)
    sibling = (at(plane, z, 1 - core), h)
    opposite = [(at(1 - plane, z, cc), h) for cc in range(2)]
    partner = (at(1 - plane, z, core), h)

    def outward(e):
        y, half, x = (h // 4 + e // 4) % 2, (h // 2 + e // 2) % 2, (h + e) % 2
        return (plane + e // 8) % 2, y * 4 + half * 2 + x

    def device(e):
        p, j = outward(e)
        return at(p, z, core), j

    buffers = (kv_0, kv_1, kv_2)

    def spot(d, whose):
        if d == 0:
            return kv_0, 0
        if d == last:
            return kv_2, len(groups[2]) - 1
        index = 2 * d - 1 + whose
        for buffer, slots, begin in zip(buffers, groups, (0, len(groups[0]), len(groups[0]) + len(groups[1]))):
            if begin <= 2 * d - 1 < begin + len(slots):
                return buffer, index - begin

    where = {slot: (buffer, n) for buffer, slots in zip(buffers, groups) for n, slot in enumerate(slots)}

    def block(slot, whose, g):
        buffer, n = where[slot]
        return buffer.at[n, whose, g]

    sides = (plane, 1 - plane)

    def granule(d, b, g):
        buffer, n = spot(d, core)
        return buffer.at[n, sides[b], g if b == 0 else (core + g) % 2]

    def own(g):
        return pltpu.make_async_copy((k_ref, v_ref)[g], granule(0, 0, g), local.at[g])

    loads = (
        pltpu.make_async_copy(q_hbm, q_ref, local.at[2]),
        pltpu.make_async_copy(layout_hbm, layout_ref, local.at[3]),
    )

    @pl.when(core == plane)
    def _():
        for g in range(2):
            own(g).start()

    for load in loads:
        load.start()

    barrier = pltpu.get_barrier_semaphore()
    around = [onward, backward, sibling, (at(1 - plane, z, 1 - core), h)] + [device(e) for e in range(1, 2 * heads)]
    for to in around:
        pl.semaphore_signal(barrier, inc=1, device_id=to, device_id_type=MESH)
    pl.semaphore_wait(barrier, len(around))

    def ring(d, b, g):
        return send(
            granule(d - 1, b, g), granule(d, b, g), ring_send.at[d - 1, b, g], ring_recv.at[d - 1, b, g], onward
        )

    def share(d, whose):
        buffer, n = spot(d, whose)
        ref = buffer.at[n, jnp.where(whose == 0, plane, 1 - plane)] if d == last else buffer.at[n]
        return send(ref, ref, share_send.at[d - 1], share_recv.at[d - 1], sibling)

    def home(g):
        return send((k_ref, v_ref)[g], granule(0, 0, g), cross_send.at[0, g], cross_recv.at[0, g], sibling)

    def abroad(g):
        return send((k_ref, v_ref)[g], kv_0.at[0, plane, g], cross_send.at[0, g], cross_recv.at[1, 0], opposite[g])

    def pass_on():
        return send(granule(0, 1, 0), granule(0, 1, 0), cross_send.at[1, 0], cross_recv.at[1, 1], sibling)

    def passed():
        return send(granule(0, 1, 1), granule(0, 1, 1), cross_send.at[1, 0], cross_recv.at[1, 1], sibling)

    def hand_over():
        return send(q_hbm, qx, first_send.at[0], first_recv.at[0], partner)

    @pl.when(core != plane)
    def _():
        for g in range(2):
            abroad(g).start()

    @pl.when(core == plane)
    def _():
        for g in range(2):
            home(g).start()

    for g in range(2):

        @pl.when(core != plane)
        def _():
            home(g).wait_recv()

        @pl.when(core == plane)
        def _():
            own(g).wait()

        ring(1, 0, g).start()
    hand_over().start()
    send(k_ref, granule(0, 1, 0), cross_send.at[0, 0], cross_recv.at[1, 0], opposite[0]).wait_recv()
    ring(1, 1, 0).start()
    pass_on().start()
    passed().wait_recv()
    ring(1, 1, 1).start()

    own_block, low_tiles, starts, tile_counts = [], [], [], []

    def arrange(slots):
        tiles, start = tiles_for(slots), sum(tile_counts) * TILE
        positions = [layout_ref[2 * ((z + nz - slot) % nz) + plane] for slot in slots]
        count = jnp.int32(0)
        for position in positions:
            count += (position <= own_block[0]).astype(jnp.int32)
        low = (count + TILE - 1) // TILE
        low_next, high_next = jnp.int32(0), low * TILE
        for n, position in enumerate(positions):
            is_low, is_high = position <= own_block[0], position >= own_block[0]
            place[0, n] = jnp.where(is_low, low_next, -1)
            place[1, n] = jnp.where(is_high, high_next, -1)
            place[2, n] = jnp.where(position == own_block[0], 0, tok)
            low_next += is_low.astype(jnp.int32)
            high_next += is_high.astype(jnp.int32)

        def order(t, _):
            index, bound = jnp.int32(0), jnp.int32(-tok)
            for n in range(len(slots)):
                here = (place[0, n] == t) | (place[1, n] == t)
                index = jnp.where(here, n, index)
                bound = jnp.where(here, place[2, n], bound)
            pick[start + t] = index
            limit[start + t] = bound
            return 0

        lax.fori_loop(0, tiles * TILE, order, 0)
        low_tiles.append(low)
        starts.append(start)
        tile_counts.append(tiles)

    def scaled(target, ref):
        for head in range(group):
            part = ref[:, head * HEAD_SIZE:(head + 1) * HEAD_SIZE].astype(jnp.float32) * SCALE
            qs[target, head] = part.astype(jnp.bfloat16)

    ones = jnp.ones((TILE * tok, HEAD_SIZE), jnp.bfloat16)

    def tile(side, keys, values, before, after, bounds, offset, count):
        values = jnp.concatenate([values, ones], axis=1)

        def scores(n):
            return lax.dot_general(
                qs[side, offset + n], keys, (((1,), (1,)), ((), ())), preferred_element_type=jnp.float32
            )

        if bounds is not None:
            ahead = lax.broadcasted_iota(jnp.int32, (tok, tok), 1) - lax.broadcasted_iota(jnp.int32, (tok, tok), 0)
        upcoming = scores(0)
        for n in range(count):
            score = upcoming
            if n + 1 < count:
                upcoming = scores(n + 1)
            parts = [score[:, j * tok:(j + 1) * tok] for j in range(TILE)]
            if bounds is not None:
                parts = [jnp.where(ahead <= bounds[j], parts[j], EMPTY) for j in range(TILE)]
            widest = parts[0]
            for part in parts[1:]:
                widest = jnp.maximum(widest, part)
            top = jnp.max(widest, axis=1, keepdims=True)
            if before is None:
                m_next = jnp.broadcast_to(top, (tok, HEAD_SIZE))
            else:
                m = m_s[before, offset + n]
                m_next = jnp.maximum(m, top)
            weight = jnp.concatenate([jnp.exp2(part - m_next).astype(jnp.bfloat16) for part in parts], axis=1)
            mixed = jnp.dot(weight, values, preferred_element_type=jnp.float32)
            if before is not None:
                factor = jnp.exp2(m - m_next)
                mixed += al_s[before, offset + n] * jnp.concatenate([factor, factor], axis=1)
            m_s[after, offset + n] = m_next
            al_s[after, offset + n] = mixed

    def first_part(slots, before, after, offset, count):
        keys = jnp.concatenate([block(slot, 0, 0)[...] for slot in slots], axis=0)
        values = jnp.concatenate([block(slot, 0, 1)[...] for slot in slots], axis=0)
        tile(1, keys, values, before, after, None, offset, count)

    def second_part(index, low_before, high_before, after, offset, count, begin=0, end=None):
        buffer, low, base, tiles = buffers[index], low_tiles[index], starts[index], tile_counts[index]

        def step(t, _):
            side = jnp.where(t < low, 0, 1)
            before = jnp.where(t == low, high_before, jnp.where(t == 0, low_before, after + t - 1))
            chosen = [pick[base + t * TILE + j] for j in range(TILE)]
            bounds = [limit[base + t * TILE + j] for j in range(TILE)]
            keys = jnp.concatenate([buffer[n, side, 0] for n in chosen], axis=0)
            values = jnp.concatenate([buffer[n, side, 1] for n in chosen], axis=0)
            tile(side, keys, values, before, after + t, bounds, offset, count)
            return 0

        lax.fori_loop(begin, tiles if end is None else end, step, 0)
        return (
            jnp.where(low == 0, low_before, after + low - 1),
            jnp.where(low == tiles, high_before, after + tiles - 1),
        )

    def shared(*steps):
        for d in steps:
            share(d, 1 - core).wait_recv()

    parts = [arrival[i:i + TILE] for i in range(0, nz, TILE)]
    ends = {}

    def lists(index):
        if index == 0:
            loads[1].wait()
            own_block.append(layout_ref[2 * z + core])
        arrange(groups[index])

    def scale_own():
        loads[0].wait()
        scaled(plane, q_ref)

    def empty_state():
        m_s[0] = jnp.full(m_s.shape[1:], EMPTY, jnp.float32)
        al_s[0] = jnp.zeros(al_s.shape[1:], jnp.float32)

    def scale_other():
        hand_over().wait_recv()
        scaled(1 - plane, qx)

    def near(begin, end):
        ends[0] = second_part(0, 0, 1, 3, 0, group, begin, end)

    def middle():
        ends[1] = second_part(1, ends[0][0], 2, 7, 0, group)

    work = {
        1: [scale_own, lambda: lists(0)],
        2: [lambda: lists(1), lambda: lists(2), empty_state],
        3: [scale_other, lambda: shared(1, 2), lambda: first_part(parts[0], None, 1, 0, group)],
        4: [lambda: shared(3), lambda: near(0, 2)],
        5: [lambda: near(2, 3), lambda: shared(4), lambda: first_part(parts[1], ends[0][1], 2, 0, group)],
        6: [lambda: shared(5), middle],
        7: [lambda: shared(6), lambda: first_part(parts[2], ends[1][1], 6, 0, group)],
    }

    for d in range(1, last + 1):
        for b in range(2):
            for g in range(2):
                if d < last:
                    ring(d, b, g).wait_recv()
                    if d + 1 < last:
                        ring(d + 1, b, g).start()
                    else:

                        @pl.when(core == b)
                        def _():
                            ring(last, b, g).start()
                else:

                    @pl.when(core == b)
                    def _():
                        ring(last, b, g).wait_recv()
                if (b, g) == (1, 1):
                    share(d, core).start()
        for task in work.get(d, ()):
            task()
    low_at, high_at = ends[1][0], 6
    shared(last - 1, last)

    lane = lax.broadcasted_iota(jnp.int32, (tok, HEAD_SIZE), 1)
    mine = plane * heads + h
    far_first = sorted(range(1, 2 * heads), key=lambda e: -(e // 8 + e // 2 % 2))

    def spread(buffer, landing, index):
        for e in far_first:
            p, j = outward(e)
            send(
                buffer.at[p * heads + j], landing.at[mine], o_send.at[index], o_recv.at[index], device(e)
            ).start()
        pltpu.make_async_copy(buffer.at[mine], landing.at[mine], o_recv.at[index]).start()

    lse[...] = jnp.zeros_like(lse)

    def chunk_step(chunk, _):
        offset = chunk * per_chunk
        first_part(parts[3], high_at, 9, offset, per_chunk)
        ends = second_part(2, low_at, 9, 10, offset, per_chunk)
        for side in range(2):
            for n in range(per_chunk):
                m, al = m_s[ends[side], offset + n], al_s[ends[side], offset + n]
                total = al[:, HEAD_SIZE:]
                some = total > 0.0
                safe = jnp.where(some, total, 1.0)
                mixed = (al[:, :HEAD_SIZE] / safe).astype(jnp.bfloat16)
                out_send[chunk, side * heads:(side + 1) * heads, :, n * HEAD_SIZE:(n + 1) * HEAD_SIZE] = (
                    mixed.reshape(heads, piece, HEAD_SIZE)
                )
                level = jnp.where(some, m + jnp.log2(safe), EMPTY)
                lse[side] = jnp.where(lax.rem(lane, group) == offset + n, level, lse[side])

        @pl.when(chunk < CHUNKS - 1)
        def _():
            spread(out_send.at[chunk], out_recv.at[chunk], chunk)

        return 0

    lax.fori_loop(0, CHUNKS, chunk_step, 0)

    for side in range(2):
        level = lse[side]
        high = level.astype(jnp.bfloat16).astype(jnp.float32)
        rest = (level - high).astype(jnp.bfloat16).astype(jnp.float32)
        low = level - high - rest
        packed = jnp.where(lane < group, high, jnp.where(lane < 2 * group, rest, low)).astype(jnp.bfloat16)
        stat_send[side * heads:(side + 1) * heads] = packed.reshape(heads, piece, HEAD_SIZE)
    spread(stat_send, stat_recv, CHUNKS)
    spread(out_send.at[CHUNKS - 1], out_recv.at[CHUNKS - 1], CHUNKS - 1)

    for d in range(1, last + 1):
        share(d, core).wait_send()
    for g in range(2):

        @pl.when(core != plane)
        def _():
            abroad(g).wait_send()

        @pl.when(core == plane)
        def _():
            home(g).wait_send()

        for b in range(2):
            for d in range(1, last):
                ring(d, b, g).wait_send()

            @pl.when(core == b)
            def _():
                ring(last, b, g).wait_send()
    pass_on().wait_send()
    hand_over().wait_send()

    pltpu.make_async_copy(stat_send, stat_recv, o_recv.at[CHUNKS]).wait()
    portions = []
    for source in range(heads):
        levels = []
        for side in range(2):
            packed = stat_recv[side * heads + source].astype(jnp.float32)
            levels.append(
                packed + pltpu.roll(packed, HEAD_SIZE - group, 1) + pltpu.roll(packed, HEAD_SIZE - 2 * group, 1)
            )
        portions.append(1.0 / (1.0 + jnp.exp2(levels[1] - levels[0])))
    for chunk in range(CHUNKS):
        pltpu.make_async_copy(out_send.at[chunk], out_recv.at[chunk], o_recv.at[chunk]).wait()
        for source in range(heads):
            for n in range(per_chunk):
                head = chunk * per_chunk + n
                columns = slice(n * HEAD_SIZE, (n + 1) * HEAD_SIZE)
                part_0 = out_recv[chunk, source, :, columns].astype(jnp.float32)
                part_1 = out_recv[chunk, heads + source, :, columns].astype(jnp.float32)
                portion = jnp.broadcast_to(portions[source][:, head:head + 1], (piece, HEAD_SIZE))
                start = (source * group + head) * HEAD_SIZE
                out_ref[:, start:start + HEAD_SIZE] = (part_1 + portion * (part_0 - part_1)).astype(jnp.bfloat16)

    others = pl.ds(0, 2 * heads - 1)
    pltpu.make_async_copy(stat_send.at[others], stat_recv.at[others], o_send.at[CHUNKS]).wait()
    for chunk in range(CHUNKS):
        pltpu.make_async_copy(out_send.at[chunk, others], out_recv.at[chunk, others], o_send.at[chunk]).wait()


def solution(mesh):
    nz, heads = mesh.shape["seq"] // 4, mesh.shape["head"]
    arrival = [0] + [slot for d in range(1, nz // 2) for slot in (d, nz - d)] + [nz // 2]
    groups = (arrival[:2 * TILE - 1], arrival[2 * TILE - 1:3 * TILE - 1], arrival[3 * TILE - 1:])

    def per_device(queries, keys, values, layout):
        tok, width = queries.shape
        group = width // HEAD_SIZE
        piece = tok // heads
        entries = sum(tiles_for(slots) for slots in groups) * TILE
        states = 1 + nz // TILE + entries // TILE
        bf16, f32, dma = jnp.bfloat16, jnp.float32, pltpu.SemaphoreType.DMA
        hbm = pl.BlockSpec(memory_space=pltpu.HBM)

        return pl.pallas_call(
            lambda *refs: kernel(nz, heads, arrival, groups, *refs),
            out_shape=jax.ShapeDtypeStruct((piece, heads * width), bf16),
            in_specs=[hbm] * 4,
            out_specs=pl.BlockSpec(memory_space=pltpu.VMEM),
            scratch_shapes=[pltpu.VMEM((len(slots), 2, 2, tok, HEAD_SIZE), bf16) for slots in groups]
            + [
                pltpu.VMEM((tok, width), bf16),
                pltpu.VMEM((tok, width), bf16),
                pltpu.VMEM((2, group, tok, HEAD_SIZE), bf16),
                pltpu.VMEM((states, group, tok, HEAD_SIZE), f32),
                pltpu.VMEM((states, group, tok, 2 * HEAD_SIZE), f32),
                pltpu.VMEM((CHUNKS, 2 * heads, piece, width // CHUNKS), bf16),
                pltpu.VMEM((CHUNKS, 2 * heads, piece, width // CHUNKS), bf16),
                pltpu.VMEM((2 * heads, piece, HEAD_SIZE), bf16),
                pltpu.VMEM((2 * heads, piece, HEAD_SIZE), bf16),
                pltpu.VMEM((2, tok, HEAD_SIZE), f32),
                pltpu.SMEM(layout.shape, jnp.int32),
                pltpu.SMEM((entries,), jnp.int32),
                pltpu.SMEM((entries,), jnp.int32),
                pltpu.SMEM((3, 2 * TILE), jnp.int32),
                dma((nz // 2, 2, 2)), dma((nz // 2, 2, 2)), dma((nz // 2,)), dma((nz // 2,)), dma((2, 2)), dma((2, 2)),
                dma((1,)), dma((1,)),
                dma((CHUNKS + 1,)), dma((CHUNKS + 1,)), dma((4,)),
            ],
            compiler_params=pltpu.CompilerParams(
                collective_id=0, has_side_effects=True, vmem_limit_bytes=44 * 1024 * 1024
            ),
            cost_estimate=pl.CostEstimate(
                flops=4 * 2 * (nz + 1) * tok * group * tok * HEAD_SIZE,
                bytes_accessed=4 * tok * width,
                transcendentals=2 * (nz + 1) * tok * group * tok,
            ),
        )(*(pltpu.with_memory_space_constraint(a, pltpu.HBM) for a in (layout, queries, keys, values)))

    return jax.shard_map(
        per_device,
        mesh=mesh,
        in_specs=(P("seq", "head"), P("seq", "head"), P("seq", "head"), P()),
        out_specs=P(("seq", "head"), None),
        check_vma=False,
    )
```
